32 devices in a mesh: row: 4 (over z), col: 8 (over y, x, core).
Axes of the slice: x: 2, y: 2, z: 4, core: 2. Of those that a mesh axis runs over, the one named last changes fastest.
Arguments:
- tiles: float32 [4, 8, 256, 128, 128], P('row', 'col'), may hold values from -0.125 to 0.125
- tile_rows: int32 [4, 8, 256], P('row', 'col'), may hold values from 0 to 127, as said below
- tile_cols: int32 [4, 8, 256], P('row', 'col'), may hold values from 0 to 63, as said below
- tile_counts: int32 [4, 8], P('row', 'col'), may hold values from 1 to 256, as said below
- block_now: float32 [8, 65536], P(None, ('row', 'col')), may hold values from -6 to 6
- block_prev: float32 [8, 65536], P(None, ('row', 'col')), may hold values from -6 to 6
- coupling: float32 [8, 8], replicated, may hold values from -3 to 3
- diag_energy: float32 [65536], P(('row', 'col')), may hold values from 1 to 4
Outputs:
- next_block: float32 [8, 65536], P(None, ('row', 'col'))
- alpha: float32 [8, 8], replicated
- beta: float32 [8, 8], replicated
The draws below stay inside these ranges and needn't reach their ends.
Inputs may be any that keep to these rules, and one draw needn't show every extreme that they name: `tile_rows`: every slot, used or not, holds a local tile row below 128; used tiles lie on or below the global diagonal. `tile_cols`: every slot holds a local tile column below 64. `tile_counts`: devices on the last block row use all 256 slots.
All inputs are finite; a program needn't handle non-finite values.
Results may differ from the reference program's by a relative error of at most 0.0003.
Values sent between devices are 32-bit elements; how exact they have to be, the bound alone decides.
No kernel may reach another device: no remote copies, remote signals or barrier semaphores. Data moves between devices by JAX's collectives and lax.ppermute only.
A program may use at most 64 MiB of HBM per device.

```python
import jax
import jax.numpy as jnp
from jax import lax

VEC = 8
TILE = 128
CHT = 16
MAXT = 256
NDIM = 65536
N_ROW = 4
N_COL = 8


def tile_layout(key):
    base_key = jax.random.fold_in(key, 4242)
    keys = jax.random.split(base_key, 4)
    shape = (N_ROW, N_COL, MAXT)
    row_tiles = N_COL * CHT
    block_row = jnp.arange(N_ROW, dtype=jnp.int32)[:, None, None]
    block_col = jnp.arange(N_COL, dtype=jnp.int32)[None, :, None]
    source_row = jax.random.randint(keys[0], shape, 0, 1 << 20) % (block_row + 1)
    within = jax.random.randint(keys[1], shape, 0, CHT)
    raw_row = jax.random.randint(keys[2], shape, 0, row_tiles)
    lowest = block_col * CHT + within
    same_row = lowest + raw_row % (row_tiles - lowest)
    local_row = jnp.where(source_row == block_row, same_row, raw_row)
    local_col = source_row * CHT + within
    share = MAXT * (jnp.arange(N_ROW, dtype=jnp.int32) + 1) // N_ROW
    jitter = jax.random.randint(keys[3], (N_ROW, N_COL), 0, max(MAXT // (2 * N_ROW), 1) + 1)
    totals = jnp.maximum(share[:, None] - jitter, 1)
    totals = jnp.where(jnp.arange(N_ROW, dtype=jnp.int32)[:, None] == N_ROW - 1, MAXT, totals)
    return (local_row.astype(jnp.int32), local_col.astype(jnp.int32), totals.astype(jnp.int32))


def draw_tile_rows(key, part):
    return tile_layout(key)[0]


def draw_tile_cols(key, part):
    return tile_layout(key)[1]


def draw_tile_counts(key, part):
    return tile_layout(key)[2]


def level_of(key, dims, pieces, low, high):
    loudness = 1.0
    for position, blocks in pieces:
        draws = jax.random.uniform(jax.random.fold_in(jax.random.fold_in(key, 6), position), (blocks,), jnp.float32, low / len(pieces), high / len(pieces))
        loudness = loudness * jnp.repeat(jnp.exp(draws), dims[position] // blocks).reshape((-1,) + (1,) * (len(dims) - 1 - position))
    return loudness


def scatter_about(rng, shape, width, bound, shards=(), kind=jnp.bfloat16):
    array = jax.random.normal(rng, shape, jnp.float32) * width
    if len(shards) > 0:
        array = level_of(rng, shape, shards, -0.22, 0.18) * array
    return jnp.clip(array, min=-bound, max=bound).astype(kind)


def setup_inputs(seed: int = 0) -> dict:
    key_list = jax.random.split(jax.random.key(seed), 9)
    tiles = scatter_about(key_list[0], (N_ROW, N_COL, MAXT, TILE, TILE), (TILE * MAXT // CHT) ** -0.5, 0.125, ((0, 4), (1, 8)), jnp.float32)
    tile_rows = draw_tile_rows(jax.random.fold_in(key_list[8], 71), 0)
    tile_cols = draw_tile_cols(jax.random.fold_in(key_list[8], 71), 0)
    tile_counts = draw_tile_counts(jax.random.fold_in(key_list[8], 71), 0)
    block_now = scatter_about(key_list[4], (VEC, NDIM), 1.0, 6.0, ((1, 32),), jnp.float32)
    block_prev = scatter_about(key_list[5], (VEC, NDIM), 1.0, 6.0, ((1, 32),), jnp.float32)
    coupling = scatter_about(key_list[6], (VEC, VEC), 0.5, 3.0, (), jnp.float32)
    diag_energy = jnp.clip(1.0 + 3.0 * jax.random.uniform(key_list[7], (NDIM,), jnp.float32) ** level_of(key_list[7], (NDIM,), ((0, 32),), -0.2, 0.2), 1.0, 4.0)
    return dict(tiles=tiles, tile_rows=tile_rows, tile_cols=tile_cols, tile_counts=tile_counts, block_now=block_now, block_prev=block_prev, coupling=coupling, diag_energy=diag_energy)


def reference(tiles, tile_rows, tile_cols, tile_counts, block_now, block_prev, coupling, diag_energy):
    vectors = block_now.shape[0]
    tile_width = tiles.shape[-1]
    slot_count = tiles.shape[2]
    vector_tiles = block_now.reshape(vectors, -1, tile_width)
    grid_rows = jnp.arange(N_ROW, dtype=jnp.int32)[:, None] * jnp.ones((1, N_COL), jnp.int32)
    grid_cols = jnp.ones((N_ROW, 1), jnp.int32) * jnp.arange(N_COL, dtype=jnp.int32)[None, :]

    def visit(image, device_item):
        tile_block, rows_local, cols_local, tile_total, block_row, block_col = device_item
        global_row = (block_row * (N_COL * CHT) + rows_local).astype(jnp.int32)
        global_col = (cols_local // CHT * (N_COL * CHT) + block_col * CHT + cols_local % CHT).astype(jnp.int32)
        alive_mask = (jnp.arange(slot_count, dtype=jnp.int32) < tile_total).astype(vector_tiles.dtype)
        col_states = vector_tiles[:, global_col, :]
        row_states = vector_tiles[:, global_row, :]
        row_terms = jnp.einsum('vmk,mjk->vmj', col_states, tile_block, precision=lax.Precision.HIGHEST) * alive_mask[None, :, None]
        column_terms = jnp.einsum('vmj,mjk->vmk', row_states, tile_block, precision=lax.Precision.HIGHEST) * alive_mask[None, :, None]
        image = image.at[:, global_row, :].add(row_terms)
        image = image.at[:, global_col, :].add(column_terms)
        return (image, None)
    items = (tiles.reshape(-1, slot_count, tile_width, tile_width), tile_rows.reshape(-1, slot_count), tile_cols.reshape(-1, slot_count), tile_counts.reshape(-1), grid_rows.reshape(-1), grid_cols.reshape(-1))
    image, _ = lax.scan(visit, jnp.zeros_like(vector_tiles), items)
    image = image.reshape(vectors, -1) + diag_energy[None, :] * block_now
    alpha = jnp.dot(block_now, image.T, precision=lax.Precision.HIGHEST) / NDIM
    residual = image - jnp.dot(alpha.T, block_now, precision=lax.Precision.HIGHEST) - jnp.dot(coupling, block_prev, precision=lax.Precision.HIGHEST)
    gram_matrix = jnp.dot(residual, residual.T, precision=lax.Precision.HIGHEST) / NDIM
    factor = jnp.linalg.cholesky(gram_matrix)
    next_block = jax.scipy.linalg.solve_triangular(factor, residual, lower=True)
    return (next_block, alpha, factor.T)
```

```python
import functools

import jax
import jax.numpy as jnp
from jax import lax
from jax.experimental import pallas as pl
from jax.experimental.pallas import tpu as pltpu
from jax.sharding import PartitionSpec as P

VMEM = pltpu.VMEM
SMEM = pltpu.SMEM
GROUP = 8
MIB = 1 << 20


def halves(x):
    high = x.astype(jnp.bfloat16)
    low = (x - high.astype(jnp.float32)).astype(jnp.bfloat16)
    return high, low


def contract(left, right):
    return lax.dot_general(
        left,
        right,
        (((1,), (1,)), ((), ())),
        precision=lax.Precision.HIGHEST,
        preferred_element_type=jnp.float32,
    )


def matmul(left, right):
    return jnp.dot(
        left, right, precision=lax.Precision.HIGHEST, preferred_element_type=jnp.float32
    )


def products_kernel(rows, planes, piece_tiles, width, *refs):
    row_idx, col_idx, count, tiles, diag = refs[:5]
    plane_in = refs[5 : 5 + planes]
    core_in = refs[5 + planes : 5 + 2 * planes]
    row_in = refs[5 + 2 * planes : 4 + 2 * planes + rows]
    keep_out, send_out, col_out, vec_rows, vec_cols, acc_rows, acc_cols = refs[
        4 + 2 * planes + rows :
    ]
    row = lax.axis_index("row")
    col = lax.axis_index("col")
    plane, core = col // 2, col % 2

    def store_split(target, base, source):
        for t in range(piece_tiles):
            high, low = halves(source[:, t * width : (t + 1) * width])
            target[base + t] = jnp.concatenate([high, low], axis=0)

    own = plane_in[0]
    for s in range(planes):
        base = jnp.bitwise_xor(plane, s) * 2 * piece_tiles
        store_split(vec_rows, base + core * piece_tiles, plane_in[s])
        store_split(vec_rows, base + (1 - core) * piece_tiles, core_in[s])
    store_split(vec_cols, row * piece_tiles, own)
    for s in range(1, rows):
        store_split(vec_cols, jnp.bitwise_xor(row, s) * piece_tiles, row_in[s - 1])
    acc_rows[...] = jnp.zeros_like(acc_rows)
    acc_cols[...] = jnp.zeros_like(acc_cols)

    total = count[0]
    spare_row = acc_rows.shape[0] - 1
    spare_col = acc_cols.shape[0] - 1

    def step(group, carry):
        for k in range(GROUP):
            m = group * GROUP + k
            alive = m < total
            r, c = row_idx[m], col_idx[m]
            high, low = halves(tiles[m])
            from_row = vec_rows[r]
            from_col = vec_cols[c]
            back = jnp.dot(
                jnp.concatenate([from_row, from_row], axis=1),
                jnp.concatenate([high, low], axis=0),
                preferred_element_type=jnp.float32,
            )
            ahead = lax.dot_general(
                jnp.concatenate([from_col, from_col], axis=1),
                jnp.concatenate([high, low], axis=1),
                (((1,), (1,)), ((), ())),
                preferred_element_type=jnp.float32,
            )
            acc_rows[jnp.where(alive, r, spare_row)] += ahead[:8] + ahead[8:]
            acc_cols[jnp.where(alive, c, spare_col)] += back[:8] + back[8:]
        return carry

    lax.fori_loop(0, (total + GROUP - 1) // GROUP, step, 0)

    for s in range(planes):
        base = jnp.bitwise_xor(plane, s) * 2 * piece_tiles
        for t in range(piece_tiles):
            at = slice(t * width, (t + 1) * width)
            keep_out[s, :, at] = acc_rows[base + core * piece_tiles + t]
            send_out[s, :, at] = acc_rows[base + (1 - core) * piece_tiles + t]
    for s in range(rows):
        base = jnp.bitwise_xor(row, s) * piece_tiles
        for t in range(piece_tiles):
            at = slice(t * width, (t + 1) * width)
            piece = acc_cols[base + t]
            if s == 0:
                piece = piece + own[:, at] * diag[:, at]
            col_out[s, :, at] = piece


def image_kernel(planes, rows, copies, *refs):
    now, prev, keep, core, cols = refs[:5]
    plane_in = refs[5 : 4 + planes]
    row_in = refs[4 + planes : 3 + planes + rows]
    image_out, sums_out = refs[3 + planes + rows :]
    image = keep[...] + core[...] + cols[...]
    for ref in plane_in + row_in:
        image = image + ref[...]
    image_out[...] = image
    block, last = now[...], prev[...]
    vectors = image.shape[0]
    both = jnp.concatenate([block, last], axis=0)
    against = contract(image, jnp.concatenate([image, both], axis=0))
    fixed = contract(both, both)
    used = against.shape[1] + 2 * fixed.shape[1]
    sums = jnp.concatenate(
        [
            against,
            fixed[:vectors],
            fixed[vectors:],
            jnp.zeros((vectors, sums_out.shape[2] - used), jnp.float32),
        ],
        axis=1,
    )
    for k in range(copies):
        sums_out[k] = sums


def finish_kernel(states, sums_in, image, now, prev, coupling, next_out, alpha_out, beta_out):
    vectors = image.shape[0]
    sums = jnp.sum(sums_in[...], axis=0) / states
    image_gram = sums[:, :vectors]
    alpha_t = sums[:, vectors : 2 * vectors]
    image_prev = sums[:, 2 * vectors : 3 * vectors]
    fixed = jnp.concatenate(
        [sums[:, 3 * vectors : 5 * vectors], sums[:, 5 * vectors : 7 * vectors]], axis=0
    )
    pair = coupling[...]
    left = jnp.concatenate([alpha_t, pair], axis=1)
    seen = jnp.concatenate([alpha_t, image_prev], axis=1)
    gram = image_gram + contract(
        jnp.concatenate([matmul(left, fixed) - seen, -left], axis=1),
        jnp.concatenate([left, seen], axis=1),
    )
    row_at = lax.broadcasted_iota(jnp.int32, (vectors, vectors), 0)
    col_at = lax.broadcasted_iota(jnp.int32, (vectors, vectors), 1)
    eye = (row_at == col_at).astype(jnp.float32)
    alpha_out[...] = contract(eye, alpha_t)
    work = jnp.concatenate([gram, eye, -left], axis=1)
    below = lax.broadcasted_iota(jnp.int32, (vectors, 1), 0)
    pivots = jnp.zeros((vectors, 1), jnp.float32)
    for j in range(vectors):
        pivot = work[j : j + 1, j : j + 1]
        line = work[j : j + 1, :]
        pivots = jnp.where(below == j, pivot, pivots)
        if j + 1 < vectors:
            factor = jnp.where(below > j, work[:, j : j + 1] / pivot, 0.0)
            work = work - factor * line
    work = work / jnp.sqrt(pivots)
    beta_out[...] = jnp.where(col_at >= row_at, work[:, :vectors], 0.0)
    next_out[...] = matmul(
        work[:, vectors:], jnp.concatenate([image[...], now[...], prev[...]], axis=0)
    )


def local(rows, cols, tiles, tile_rows, tile_cols, tile_counts, block_now, block_prev, coupling, diag_energy):
    slots, width = tiles.shape[2], tiles.shape[4]
    vectors, piece = block_now.shape
    piece_tiles = piece // width
    planes = cols // 2
    f32 = jnp.float32
    piece_shape = jax.ShapeDtypeStruct((vectors, piece), f32)

    def along_col(x, s):
        return lax.ppermute(x, "col", [(i, i ^ s) for i in range(cols)])

    def along_row(x, s):
        return lax.ppermute(x, "row", [(i, i ^ s) for i in range(rows)])

    row_in = [along_row(block_now, s) for s in range(1, rows)]
    plane_in = [block_now] + [along_col(block_now, 2 * s) for s in range(1, planes)]
    core_in = [along_col(x, 1) for x in plane_in]

    in_vmem = pl.BlockSpec(memory_space=VMEM)
    in_smem = pl.BlockSpec(memory_space=SMEM)
    held = pltpu.with_memory_space_constraint(tiles.reshape(slots, width, width), VMEM)
    keep, send, col_parts = pl.pallas_call(
        functools.partial(products_kernel, rows, planes, piece_tiles, width),
        out_shape=(
            jax.ShapeDtypeStruct((planes, vectors, piece), f32),
            jax.ShapeDtypeStruct((planes, vectors, piece), f32),
            jax.ShapeDtypeStruct((rows, vectors, piece), f32),
        ),
        in_specs=[in_smem] * 3 + [in_vmem] * (2 * planes + rows + 1),
        out_specs=(in_vmem,) * 3,
        scratch_shapes=[
            VMEM((cols * piece_tiles, 2 * vectors, width), jnp.bfloat16),
            VMEM((rows * piece_tiles, 2 * vectors, width), jnp.bfloat16),
            VMEM((cols * piece_tiles + 1, vectors, width), f32),
            VMEM((rows * piece_tiles + 1, vectors, width), f32),
        ],
        compiler_params=pltpu.CompilerParams(vmem_limit_bytes=24 * MIB),
        name="products",
    )(
        tile_rows.reshape(slots),
        tile_cols.reshape(slots),
        tile_counts.reshape(1),
        held,
        diag_energy.reshape(1, piece),
        *plane_in,
        *core_in,
        *row_in,
    )

    back_rows = [along_row(col_parts[s], s) for s in range(1, rows)]
    from_core = along_col(send, 1)
    summed = [keep[s] + from_core[s] for s in range(1, planes)]
    back_planes = [along_col(summed[s - 1], 2 * s) for s in range(1, planes)]

    devices = rows * cols
    image, sums = pl.pallas_call(
        functools.partial(image_kernel, planes, rows, devices),
        out_shape=(piece_shape, jax.ShapeDtypeStruct((devices, vectors, 128), f32)),
        in_specs=[in_vmem] * (3 + planes + rows),
        out_specs=(in_vmem,) * 2,
        compiler_params=pltpu.CompilerParams(vmem_limit_bytes=16 * MIB),
        name="image",
    )(block_now, block_prev, keep[0], from_core[0], col_parts[0], *back_planes, *back_rows)

    sums = lax.all_to_all(sums, ("row", "col"), 0, 0)
    return pl.pallas_call(
        functools.partial(finish_kernel, float(piece * devices)),
        out_shape=(
            piece_shape,
            jax.ShapeDtypeStruct((vectors, vectors), f32),
            jax.ShapeDtypeStruct((vectors, vectors), f32),
        ),
        in_specs=[in_vmem] * 5,
        out_specs=(in_vmem,) * 3,
        compiler_params=pltpu.CompilerParams(vmem_limit_bytes=16 * MIB),
        name="finish",
    )(sums, image, block_now, block_prev, coupling)


def solution(mesh):
    return jax.shard_map(
        functools.partial(local, mesh.shape["row"], mesh.shape["col"]),
        mesh=mesh,
        in_specs=(
            P("row", "col", None, None, None),
            P("row", "col", None),
            P("row", "col", None),
            P("row", "col"),
            P(None, ("row", "col")),
            P(None, ("row", "col")),
            P(),
            P(("row", "col")),
        ),
        out_specs=(P(None, ("row", "col")), P(), P()),
        check_vma=False,
    )
```

```python
import functools
import math

import jax
import jax.numpy as jnp
from jax import lax
from jax.experimental import pallas as pl
from jax.experimental.pallas import tpu as pltpu
from jax.sharding import PartitionSpec as P

VMEM = pltpu.VMEM
SMEM = pltpu.SMEM
GROUP = 32
MIB = 1 << 20


def halves(x):
    high = x.astype(jnp.bfloat16)
    low = (x - high.astype(jnp.float32)).astype(jnp.bfloat16)
    return high, low


def contract(left, right):
    return lax.dot_general(
        left,
        right,
        (((1,), (1,)), ((), ())),
        precision=lax.Precision.HIGHEST,
        preferred_element_type=jnp.float32,
    )


def matmul(left, right):
    return jnp.dot(
        left, right, precision=lax.Precision.HIGHEST, preferred_element_type=jnp.float32
    )


def products_kernel(rows, planes, group, *refs):
    tiles_hbm, row_idx_hbm, col_idx_hbm, count_hbm, diag_hbm, own_hbm = refs[:6]
    refs = refs[6:]
    plane_in = refs[: planes - 1]
    core_in = refs[planes - 1 : 2 * planes - 1]
    row_in = refs[2 * planes - 1 : 2 * planes + rows - 2]
    (
        keep_out,
        send_out,
        col_out,
        tiles,
        row_idx,
        col_idx,
        count,
        diag,
        own,
        vec_rows,
        vec_cols,
        acc_rows,
        acc_cols,
        small_sems,
        tile_sems,
    ) = refs[2 * planes + rows - 2 :]
    row = lax.axis_index("row")
    col = lax.axis_index("col")
    plane, core = col // 2, col % 2
    width = tiles.shape[-1]
    piece_tiles = own.shape[1] // width

    small = [
        pltpu.make_async_copy(source, target, small_sems.at[k])
        for k, (source, target) in enumerate(
            (
                (count_hbm, count),
                (row_idx_hbm, row_idx),
                (col_idx_hbm, col_idx),
                (own_hbm, own),
                (diag_hbm, diag),
            )
        )
    ]

    def tile_copy(g):
        at = pl.ds(g * group, group)
        return pltpu.make_async_copy(tiles_hbm.at[at], tiles.at[at], tile_sems.at[g])

    for copy in small:
        copy.start()
    small[0].wait()
    total = count[0, 0]
    groups = (total + group - 1) // group

    def start_tiles(g, carry):
        tile_copy(g).start()
        return carry

    lax.fori_loop(0, groups, start_tiles, 0)
    acc_rows[...] = jnp.zeros_like(acc_rows)
    acc_cols[...] = jnp.zeros_like(acc_cols)

    def store_split(target, base, source):
        for t in range(piece_tiles):
            high, low = halves(source[:, t * width : (t + 1) * width])
            target[base + t] = jnp.concatenate([high, low], axis=0)

    for s in range(1, planes):
        base = jnp.bitwise_xor(plane, s) * 2 * piece_tiles
        store_split(vec_rows, base + core * piece_tiles, plane_in[s - 1])
    for s in range(planes):
        base = jnp.bitwise_xor(plane, s) * 2 * piece_tiles
        store_split(vec_rows, base + (1 - core) * piece_tiles, core_in[s])
    for s in range(1, rows):
        store_split(vec_cols, jnp.bitwise_xor(row, s) * piece_tiles, row_in[s - 1])
    for copy in small[1:]:
        copy.wait()
    store_split(vec_rows, col * piece_tiles, own)
    store_split(vec_cols, row * piece_tiles, own)

    spare_row = acc_rows.shape[0] - 1
    spare_col = acc_cols.shape[0] - 1

    def step(g, carry):
        tile_copy(g).wait()
        for k in range(group):
            m = g * group + k
            alive = m < total
            r, c = row_idx[0, 0, m], col_idx[0, 0, m]
            high, low = halves(tiles[m])
            from_row = vec_rows[r]
            from_col = vec_cols[c]
            back = jnp.dot(
                jnp.concatenate([from_row, from_row], axis=1),
                jnp.concatenate([high, low], axis=0),
                preferred_element_type=jnp.float32,
            )
            ahead = lax.dot_general(
                jnp.concatenate([high, low], axis=1),
                jnp.concatenate([from_col, from_col], axis=1),
                (((1,), (1,)), ((), ())),
                preferred_element_type=jnp.float32,
            ).T
            acc_rows[jnp.where(alive, r, spare_row)] += ahead[:8] + ahead[8:]
            acc_cols[jnp.where(alive, c, spare_col)] += back[:8] + back[8:]
        return carry

    lax.fori_loop(0, groups, step, 0)

    for s in range(planes):
        base = jnp.bitwise_xor(plane, s) * 2 * piece_tiles
        for t in range(piece_tiles):
            at = slice(t * width, (t + 1) * width)
            keep_out[s, :, at] = acc_rows[base + core * piece_tiles + t]
            send_out[s, :, at] = acc_rows[base + (1 - core) * piece_tiles + t]
    for s in range(rows):
        base = jnp.bitwise_xor(row, s) * piece_tiles
        for t in range(piece_tiles):
            at = slice(t * width, (t + 1) * width)
            piece = acc_cols[base + t]
            if s == 0:
                piece = piece + own[:, at] * diag[:, at]
            col_out[s, :, at] = piece


def image_kernel(planes, rows, copies, *refs):
    now, prev, keep, core, cols = refs[:5]
    plane_in = refs[5 : 4 + planes]
    row_in = refs[4 + planes : 3 + planes + rows]
    image_out, sums_out = refs[3 + planes + rows :]
    image = keep[...] + core[...] + cols[...]
    for ref in plane_in + row_in:
        image = image + ref[...]
    image_out[...] = image
    block, last = now[...], prev[...]
    vectors = image.shape[0]
    both = jnp.concatenate([block, last], axis=0)
    against = contract(image, jnp.concatenate([image, both], axis=0))
    fixed = contract(both, both)
    used = against.shape[1] + 2 * fixed.shape[1]
    sums = jnp.concatenate(
        [
            against,
            fixed[:vectors],
            fixed[vectors:],
            jnp.zeros((vectors, sums_out.shape[2] - used), jnp.float32),
        ],
        axis=1,
    )
    for k in range(copies):
        sums_out[k] = sums


def finish_kernel(states, sums_in, image, now, prev, coupling, next_out, alpha_out, beta_out):
    vectors = image.shape[0]
    sums = jnp.sum(sums_in[...], axis=0) / states
    image_gram = sums[:, :vectors]
    alpha_t = sums[:, vectors : 2 * vectors]
    image_prev = sums[:, 2 * vectors : 3 * vectors]
    fixed = jnp.concatenate(
        [sums[:, 3 * vectors : 5 * vectors], sums[:, 5 * vectors : 7 * vectors]], axis=0
    )
    pair = coupling[...]
    left = jnp.concatenate([alpha_t, pair], axis=1)
    seen = jnp.concatenate([alpha_t, image_prev], axis=1)
    gram = image_gram + contract(
        jnp.concatenate([matmul(left, fixed) - seen, -left], axis=1),
        jnp.concatenate([left, seen], axis=1),
    )
    row_at = lax.broadcasted_iota(jnp.int32, (vectors, vectors), 0)
    col_at = lax.broadcasted_iota(jnp.int32, (vectors, vectors), 1)
    eye = (row_at == col_at).astype(jnp.float32)
    alpha_out[...] = contract(eye, alpha_t)
    work = jnp.concatenate([gram, eye, -left], axis=1)
    below = lax.broadcasted_iota(jnp.int32, (vectors, 1), 0)
    pivots = jnp.zeros((vectors, 1), jnp.float32)
    for j in range(vectors):
        pivot = work[j : j + 1, j : j + 1]
        line = work[j : j + 1, :]
        pivots = jnp.where(below == j, pivot, pivots)
        if j + 1 < vectors:
            factor = jnp.where(below > j, work[:, j : j + 1] / pivot, 0.0)
            work = work - factor * line
    work = work / jnp.sqrt(pivots)
    beta_out[...] = jnp.where(col_at >= row_at, work[:, :vectors], 0.0)
    next_out[...] = matmul(
        work[:, vectors:], jnp.concatenate([image[...], now[...], prev[...]], axis=0)
    )


def local(rows, cols, tiles, tile_rows, tile_cols, tile_counts, block_now, block_prev, coupling, diag_energy):
    slots, width = tiles.shape[2], tiles.shape[4]
    vectors, piece = block_now.shape
    piece_tiles = piece // width
    planes = cols // 2
    f32 = jnp.float32
    piece_shape = jax.ShapeDtypeStruct((vectors, piece), f32)

    def along_col(x, s):
        return lax.ppermute(x, "col", [(i, i ^ s) for i in range(cols)])

    def along_row(x, s):
        return lax.ppermute(x, "row", [(i, i ^ s) for i in range(rows)])

    row_in = [along_row(block_now, s) for s in range(1, rows)]
    plane_in = [block_now] + [along_col(block_now, 2 * s) for s in range(1, planes)]
    core_in = [along_col(x, 1) for x in plane_in]

    in_vmem = pl.BlockSpec(memory_space=VMEM)
    in_hbm = pl.BlockSpec(memory_space=pltpu.HBM)
    group = math.gcd(slots, GROUP)

    def stay(x):
        return pltpu.with_memory_space_constraint(x, pltpu.HBM)

    keep, send, col_parts = pl.pallas_call(
        functools.partial(products_kernel, rows, planes, group),
        out_shape=(
            jax.ShapeDtypeStruct((planes, vectors, piece), f32),
            jax.ShapeDtypeStruct((planes, vectors, piece), f32),
            jax.ShapeDtypeStruct((rows, vectors, piece), f32),
        ),
        in_specs=[in_hbm] * 3 + [pl.BlockSpec(memory_space=pl.ANY)] + [in_hbm] * 2 + [in_vmem] * (2 * planes + rows - 2),
        out_specs=(in_vmem,) * 3,
        scratch_shapes=[
            VMEM((slots, width, width), f32),
            SMEM(tile_rows.shape, jnp.int32),
            SMEM(tile_cols.shape, jnp.int32),
            SMEM(tile_counts.shape, jnp.int32),
            VMEM((1, piece), f32),
            VMEM((vectors, piece), f32),
            VMEM((cols * piece_tiles, 2 * vectors, width), jnp.bfloat16),
            VMEM((rows * piece_tiles, 2 * vectors, width), jnp.bfloat16),
            VMEM((cols * piece_tiles + 1, vectors, width), f32),
            VMEM((rows * piece_tiles + 1, vectors, width), f32),
            pltpu.SemaphoreType.DMA((5,)),
            pltpu.SemaphoreType.DMA((slots // group,)),
        ],
        compiler_params=pltpu.CompilerParams(vmem_limit_bytes=40 * MIB),
        name="products",
    )(
        stay(tiles.reshape(slots, width, width)),
        stay(tile_rows),
        stay(tile_cols),
        tile_counts,
        stay(diag_energy.reshape(1, piece)),
        stay(block_now),
        *plane_in[1:],
        *core_in,
        *row_in,
    )

    back_rows = [along_row(col_parts[s], s) for s in range(1, rows)]
    from_core = along_col(send, 1)
    summed = [keep[s] + from_core[s] for s in range(1, planes)]
    back_planes = [along_col(summed[s - 1], 2 * s) for s in range(1, planes)]

    devices = rows * cols
    image, sums = pl.pallas_call(
        functools.partial(image_kernel, planes, rows, devices),
        out_shape=(piece_shape, jax.ShapeDtypeStruct((devices, vectors, 128), f32)),
        in_specs=[in_vmem] * (3 + planes + rows),
        out_specs=(in_vmem,) * 2,
        compiler_params=pltpu.CompilerParams(vmem_limit_bytes=16 * MIB),
        name="image",
    )(block_now, block_prev, keep[0], from_core[0], col_parts[0], *back_planes, *back_rows)

    sums = lax.all_to_all(sums, ("row", "col"), 0, 0)
    return pl.pallas_call(
        functools.partial(finish_kernel, float(piece * devices)),
        out_shape=(
            piece_shape,
            jax.ShapeDtypeStruct((vectors, vectors), f32),
            jax.ShapeDtypeStruct((vectors, vectors), f32),
        ),
        in_specs=[in_vmem] * 5,
        out_specs=(in_vmem,) * 3,
        compiler_params=pltpu.CompilerParams(vmem_limit_bytes=16 * MIB),
        name="finish",
    )(sums, image, block_now, block_prev, coupling)


def solution(mesh):
    return jax.shard_map(
        functools.partial(local, mesh.shape["row"], mesh.shape["col"]),
        mesh=mesh,
        in_specs=(
            P("row", "col", None, None, None),
            P("row", "col", None),
            P("row", "col", None),
            P("row", "col"),
            P(None, ("row", "col")),
            P(None, ("row", "col")),
            P(),
            P(("row", "col")),
        ),
        out_specs=(P(None, ("row", "col")), P(), P()),
        check_vma=False,
    )
```

```python
import functools
import math

import jax
import jax.numpy as jnp
from jax import lax
from jax.experimental import pallas as pl
from jax.experimental.pallas import tpu as pltpu
from jax.sharding import PartitionSpec as P

VMEM = pltpu.VMEM
SMEM = pltpu.SMEM
GROUP = 32
MIB = 1 << 20


def pair_steps(count):
    last = [0] * count
    steps = []
    for high in range(1, count):
        for low in range(high):
            at = max(last[low], last[high])
            last[low] = last[high] = at + 1
            if at == len(steps):
                steps.append(list(range(count)))
            steps[at][low], steps[at][high] = high, low
    return steps


def partner(step, mine):
    found = jnp.int32(step[0])
    for k in range(1, len(step)):
        found = jnp.where(mine == k, step[k], found)
    return found


def halves(x):
    high = x.astype(jnp.bfloat16)
    low = (x - high.astype(jnp.float32)).astype(jnp.bfloat16)
    return high, low


def contract(left, right):
    return lax.dot_general(
        left,
        right,
        (((1,), (1,)), ((), ())),
        precision=lax.Precision.HIGHEST,
        preferred_element_type=jnp.float32,
    )


def matmul(left, right):
    return jnp.dot(
        left, right, precision=lax.Precision.HIGHEST, preferred_element_type=jnp.float32
    )


def products_kernel(steps, planes, group, *refs):
    count, tiles_hbm, row_idx_hbm, col_idx_hbm, diag_hbm, own_hbm = refs[:6]
    refs = refs[6:]
    plane_in = refs[: planes - 1]
    core_in = refs[planes - 1 : 2 * planes - 1]
    row_in = refs[2 * planes - 1 : 2 * planes - 1 + len(steps)]
    (
        keep_out,
        send_out,
        col_own,
        col_out,
        tiles,
        row_idx,
        col_idx,
        diag,
        own,
        vec_rows,
        vec_cols,
        acc_rows,
        acc_cols,
        small_sems,
        tile_sems,
    ) = refs[2 * planes - 1 + len(steps) :]
    row = lax.axis_index("row")
    col = lax.axis_index("col")
    plane, core = col // 2, col % 2
    width = tiles.shape[-1]
    piece_tiles = own.shape[1] // width

    small = [
        pltpu.make_async_copy(source, target, small_sems.at[k])
        for k, (source, target) in enumerate(
            (
                (row_idx_hbm, row_idx),
                (col_idx_hbm, col_idx),
                (own_hbm, own),
                (diag_hbm, diag),
            )
        )
    ]

    def tile_copy(g):
        at = pl.ds(g * group, group)
        return pltpu.make_async_copy(tiles_hbm.at[at], tiles.at[at], tile_sems.at[g])

    total = count[0, 0]
    groups = (total + group - 1) // group

    def start_tiles(g, carry):
        tile_copy(g).start()
        return carry

    tile_copy(0).start()
    for copy in small:
        copy.start()
    lax.fori_loop(1, groups, start_tiles, 0)
    acc_rows[...] = jnp.zeros_like(acc_rows)
    acc_cols[...] = jnp.zeros_like(acc_cols)

    def store_split(target, base, source):
        for t in range(piece_tiles):
            high, low = halves(source[:, t * width : (t + 1) * width])
            target[base + t] = jnp.concatenate([high, low], axis=0)

    for s in range(1, planes):
        base = jnp.bitwise_xor(plane, s) * 2 * piece_tiles
        store_split(vec_rows, base + core * piece_tiles, plane_in[s - 1])
    for s in range(planes):
        base = jnp.bitwise_xor(plane, s) * 2 * piece_tiles
        store_split(vec_rows, base + (1 - core) * piece_tiles, core_in[s])
    for step, source in zip(steps, row_in):
        store_split(vec_cols, partner(step, row) * piece_tiles, source)
    for copy in small:
        copy.wait()
    store_split(vec_rows, col * piece_tiles, own)
    store_split(vec_cols, row * piece_tiles, own)

    spare_row = acc_rows.shape[0] - 1
    spare_col = acc_cols.shape[0] - 1

    def multiply(g, carry):
        tile_copy(g).wait()
        for k in range(group):
            m = g * group + k
            alive = m < total
            r, c = row_idx[0, 0, m], col_idx[0, 0, m]
            high, low = halves(tiles[m])
            from_row = vec_rows[r]
            from_col = vec_cols[c]
            back = jnp.dot(
                jnp.concatenate([from_row, from_row], axis=1),
                jnp.concatenate([high, low], axis=0),
                preferred_element_type=jnp.float32,
            )
            ahead = lax.dot_general(
                jnp.concatenate([high, low], axis=1),
                jnp.concatenate([from_col, from_col], axis=1),
                (((1,), (1,)), ((), ())),
                preferred_element_type=jnp.float32,
            ).T
            acc_rows[jnp.where(alive, r, spare_row)] += ahead[:8] + ahead[8:]
            acc_cols[jnp.where(alive, c, spare_col)] += back[:8] + back[8:]
        return carry

    lax.fori_loop(0, groups, multiply, 0)

    for s in range(planes):
        base = jnp.bitwise_xor(plane, s) * 2 * piece_tiles
        for t in range(piece_tiles):
            at = slice(t * width, (t + 1) * width)
            keep_out[s, :, at] = acc_rows[base + core * piece_tiles + t]
            send_out[s, :, at] = acc_rows[base + (1 - core) * piece_tiles + t]
    for t in range(piece_tiles):
        at = slice(t * width, (t + 1) * width)
        col_own[:, at] = acc_cols[row * piece_tiles + t] + own[:, at] * diag[:, at]
    for k, step in enumerate(steps):
        other = partner(step, row)
        base = other * piece_tiles
        for t in range(piece_tiles):
            at = slice(t * width, (t + 1) * width)
            col_out[k, :, at] = jnp.where(other == row, 0.0, acc_cols[base + t])


def image_kernel(copies, *refs):
    now, prev = refs[:2]
    image_out, sums_out = refs[-2:]
    image = refs[2][...]
    for ref in refs[3:-2]:
        image = image + ref[...]
    image_out[...] = image
    block, last = now[...], prev[...]
    vectors = image.shape[0]
    both = jnp.concatenate([block, last], axis=0)
    against = contract(image, jnp.concatenate([image, both], axis=0))
    fixed = contract(both, both)
    half = sums_out.shape[2] // 2
    used = against.shape[1] + 2 * fixed.shape[1]
    sums = jnp.concatenate(
        [
            against,
            fixed[:vectors],
            fixed[vectors:],
            jnp.zeros((vectors, half - used), jnp.float32),
        ],
        axis=1,
    )
    sums = jnp.concatenate([sums[: vectors // 2], sums[vectors // 2 :]], axis=1)
    for k in range(copies):
        sums_out[k] = sums


def finish_kernel(states, sums_in, image, now, prev, coupling, next_out, alpha_out, beta_out):
    vectors = image.shape[0]
    sums = jnp.sum(sums_in[...], axis=0) / states
    half = sums.shape[1] // 2
    sums = jnp.concatenate([sums[:, :half], sums[:, half:]], axis=0)
    image_gram = sums[:, :vectors]
    alpha_t = sums[:, vectors : 2 * vectors]
    image_prev = sums[:, 2 * vectors : 3 * vectors]
    fixed = jnp.concatenate(
        [sums[:, 3 * vectors : 5 * vectors], sums[:, 5 * vectors : 7 * vectors]], axis=0
    )
    pair = coupling[...]
    left = jnp.concatenate([alpha_t, pair], axis=1)
    seen = jnp.concatenate([alpha_t, image_prev], axis=1)
    gram = image_gram + contract(
        jnp.concatenate([matmul(left, fixed) - seen, -left], axis=1),
        jnp.concatenate([left, seen], axis=1),
    )
    row_at = lax.broadcasted_iota(jnp.int32, (vectors, vectors), 0)
    col_at = lax.broadcasted_iota(jnp.int32, (vectors, vectors), 1)
    eye = (row_at == col_at).astype(jnp.float32)
    alpha_out[...] = contract(eye, alpha_t)
    work = jnp.concatenate([gram, eye, -left], axis=1)
    below = lax.broadcasted_iota(jnp.int32, (vectors, 1), 0)
    pivots = jnp.zeros((vectors, 1), jnp.float32)
    for j in range(vectors):
        pivot = work[j : j + 1, j : j + 1]
        line = work[j : j + 1, :]
        pivots = jnp.where(below == j, pivot, pivots)
        if j + 1 < vectors:
            factor = jnp.where(below > j, work[:, j : j + 1] / pivot, 0.0)
            work = work - factor * line
    work = work / jnp.sqrt(pivots)
    beta_out[...] = jnp.where(col_at >= row_at, work[:, :vectors], 0.0)
    next_out[...] = matmul(
        work[:, vectors:], jnp.concatenate([image[...], now[...], prev[...]], axis=0)
    )


def local(rows, cols, tiles, tile_rows, tile_cols, tile_counts, block_now, block_prev, coupling, diag_energy):
    slots, width = tiles.shape[2], tiles.shape[4]
    vectors, piece = block_now.shape
    piece_tiles = piece // width
    planes = cols // 2
    f32 = jnp.float32
    piece_shape = jax.ShapeDtypeStruct((vectors, piece), f32)

    def along_col(x, s):
        return lax.ppermute(x, "col", [(i, i ^ s) for i in range(cols)])

    def along_row(x, step):
        return lax.ppermute(x, "row", list(enumerate(step)))

    steps = pair_steps(rows)[::-1]
    row_in = [along_row(block_now, step) for step in steps]
    plane_in = [block_now] + [along_col(block_now, 2 * s) for s in range(1, planes)]
    core_in = [along_col(x, 1) for x in plane_in]

    in_vmem = pl.BlockSpec(memory_space=VMEM)
    in_hbm = pl.BlockSpec(memory_space=pltpu.HBM)
    group = math.gcd(slots, GROUP)

    def stay(x):
        return pltpu.with_memory_space_constraint(x, pltpu.HBM)

    keep, send, col_own, col_parts = pl.pallas_call(
        functools.partial(products_kernel, steps, planes, group),
        out_shape=(
            jax.ShapeDtypeStruct((planes, vectors, piece), f32),
            jax.ShapeDtypeStruct((planes, vectors, piece), f32),
            piece_shape,
            jax.ShapeDtypeStruct((len(steps), vectors, piece), f32),
        ),
        in_specs=[pl.BlockSpec(memory_space=SMEM)]
        + [in_hbm] * 5
        + [in_vmem] * (2 * planes - 1 + len(steps)),
        out_specs=(in_vmem,) * 4,
        scratch_shapes=[
            VMEM((slots, width, width), f32),
            SMEM(tile_rows.shape, jnp.int32),
            SMEM(tile_cols.shape, jnp.int32),
            VMEM((1, piece), f32),
            VMEM((vectors, piece), f32),
            VMEM((cols * piece_tiles, 2 * vectors, width), jnp.bfloat16),
            VMEM((rows * piece_tiles, 2 * vectors, width), jnp.bfloat16),
            VMEM((cols * piece_tiles + 1, vectors, width), f32),
            VMEM((rows * piece_tiles + 1, vectors, width), f32),
            pltpu.SemaphoreType.DMA((4,)),
            pltpu.SemaphoreType.DMA((slots // group,)),
        ],
        compiler_params=pltpu.CompilerParams(vmem_limit_bytes=40 * MIB),
        name="products",
    )(
        tile_counts,
        stay(tiles.reshape(slots, width, width)),
        stay(tile_rows),
        stay(tile_cols),
        stay(diag_energy.reshape(1, piece)),
        stay(block_now),
        *plane_in[1:],
        *core_in,
        *row_in,
    )

    back_rows = [along_row(col_parts[k], step) for k, step in enumerate(steps)]
    from_core = along_col(send, 1)
    summed = [keep[s] + from_core[s] for s in range(1, planes)]
    back_planes = [along_col(summed[s - 1], 2 * s) for s in range(1, planes)]
    terms = [keep[0], from_core[0], col_own, *back_planes, *back_rows]

    devices = rows * cols
    image, sums = pl.pallas_call(
        functools.partial(image_kernel, devices),
        out_shape=(
            piece_shape,
            jax.ShapeDtypeStruct((devices, vectors // 2, 128), f32),
        ),
        in_specs=[in_vmem] * (2 + len(terms)),
        out_specs=(in_vmem,) * 2,
        compiler_params=pltpu.CompilerParams(vmem_limit_bytes=16 * MIB),
        name="image",
    )(block_now, block_prev, *terms)

    sums = lax.all_to_all(sums, ("row", "col"), 0, 0)
    return pl.pallas_call(
        functools.partial(finish_kernel, float(piece * devices)),
        out_shape=(
            piece_shape,
            jax.ShapeDtypeStruct((vectors, vectors), f32),
            jax.ShapeDtypeStruct((vectors, vectors), f32),
        ),
        in_specs=[in_vmem] * 5,
        out_specs=(in_vmem,) * 3,
        compiler_params=pltpu.CompilerParams(vmem_limit_bytes=16 * MIB),
        name="finish",
    )(sums, image, block_now, block_prev, coupling)


def solution(mesh):
    return jax.shard_map(
        functools.partial(local, mesh.shape["row"], mesh.shape["col"]),
        mesh=mesh,
        in_specs=(
            P("row", "col", None, None, None),
            P("row", "col", None),
            P("row", "col", None),
            P("row", "col"),
            P(None, ("row", "col")),
            P(None, ("row", "col")),
            P(),
            P(("row", "col")),
        ),
        out_specs=(P(None, ("row", "col")), P(), P()),
        check_vma=False,
    )
```

```python
import functools
import math

import jax
import jax.numpy as jnp
from jax import lax
from jax.experimental import pallas as pl
from jax.experimental.pallas import tpu as pltpu
from jax.sharding import PartitionSpec as P

VMEM = pltpu.VMEM
SMEM = pltpu.SMEM
GROUP = 32
MIB = 1 << 20


def halves(x):
    high = x.astype(jnp.bfloat16)
    low = (x - high.astype(jnp.float32)).astype(jnp.bfloat16)
    return high, low


def contract(left, right):
    return lax.dot_general(
        left,
        right,
        (((1,), (1,)), ((), ())),
        precision=lax.Precision.HIGHEST,
        preferred_element_type=jnp.float32,
    )


def matmul(left, right):
    return jnp.dot(
        left, right, precision=lax.Precision.HIGHEST, preferred_element_type=jnp.float32
    )


def products_kernel(rows, planes, group, *refs):
    peers = max(planes, rows) - 1
    count, tiles_hbm, row_idx_hbm, col_idx_hbm, diag_hbm, own_hbm, beside = refs[:7]
    fetched = refs[7 : 7 + peers]
    passed = refs[7 + peers : 7 + 2 * peers]
    (
        keep_out,
        send_out,
        col_out,
        tiles,
        row_idx,
        col_idx,
        diag,
        own,
        vec_rows,
        vec_cols,
        acc_rows,
        acc_cols,
        small_sems,
        tile_sems,
    ) = refs[7 + 2 * peers :]
    row = lax.axis_index("row")
    col = lax.axis_index("col")
    plane, core = col // 2, col % 2
    vectors = own.shape[0]
    width = tiles.shape[-1]
    piece_tiles = own.shape[1] // width
    first = core == 0

    small = [
        pltpu.make_async_copy(source, target, small_sems.at[k])
        for k, (source, target) in enumerate(
            (
                (row_idx_hbm, row_idx),
                (col_idx_hbm, col_idx),
                (own_hbm, own),
                (diag_hbm, diag),
            )
        )
    ]

    def tile_copy(g):
        at = pl.ds(g * group, group)
        return pltpu.make_async_copy(tiles_hbm.at[at], tiles.at[at], tile_sems.at[g])

    total = count[0, 0]
    groups = (total + group - 1) // group

    def start_tiles(g, carry):
        tile_copy(g).start()
        return carry

    tile_copy(0).start()
    for copy in small:
        copy.start()
    lax.fori_loop(1, groups, start_tiles, 0)
    acc_rows[...] = jnp.zeros_like(acc_rows)
    acc_cols[...] = jnp.zeros_like(acc_cols)

    def store_split(target, base, read):
        for t in range(piece_tiles):
            high, low = halves(read(slice(t * width, (t + 1) * width)))
            target[base + t] = jnp.concatenate([high, low], axis=0)

    for s in range(1, planes):
        base = jnp.bitwise_xor(plane, s) * 2 * piece_tiles
        for side in range(2):
            part = slice(side * vectors, (side + 1) * vectors)
            store_split(
                vec_rows,
                base + side * piece_tiles,
                lambda at: jnp.where(first, fetched[s - 1][part, at], passed[s - 1][part, at]),
            )
    for s in range(1, rows):
        store_split(
            vec_cols,
            jnp.bitwise_xor(row, s) * piece_tiles,
            lambda at: jnp.where(
                first, passed[s - 1][vectors:, at], fetched[s - 1][:vectors, at]
            ),
        )
    store_split(vec_rows, (col + 1 - 2 * core) * piece_tiles, lambda at: beside[:, at])
    for copy in small:
        copy.wait()
    store_split(vec_rows, col * piece_tiles, lambda at: own[:, at])
    store_split(vec_cols, row * piece_tiles, lambda at: own[:, at])

    spare_row = acc_rows.shape[0] - 1
    spare_col = acc_cols.shape[0] - 1

    def multiply(g, carry):
        tile_copy(g).wait()
        for k in range(group):
            m = g * group + k
            alive = m < total
            r, c = row_idx[0, 0, m], col_idx[0, 0, m]
            high, low = halves(tiles[m])
            from_row = vec_rows[r]
            from_col = vec_cols[c]
            back = jnp.dot(
                jnp.concatenate([from_row, from_row], axis=1),
                jnp.concatenate([high, low], axis=0),
                preferred_element_type=jnp.float32,
            )
            ahead = lax.dot_general(
                jnp.concatenate([high, low], axis=1),
                jnp.concatenate([from_col, from_col], axis=1),
                (((1,), (1,)), ((), ())),
                preferred_element_type=jnp.float32,
            ).T
            acc_rows[jnp.where(alive, r, spare_row)] += ahead[:8] + ahead[8:]
            acc_cols[jnp.where(alive, c, spare_col)] += back[:8] + back[8:]
        return carry

    lax.fori_loop(0, groups, multiply, 0)

    for s in range(planes):
        base = jnp.bitwise_xor(plane, s) * 2 * piece_tiles
        for t in range(piece_tiles):
            at = slice(t * width, (t + 1) * width)
            keep_out[s, :, at] = acc_rows[base + core * piece_tiles + t]
            send_out[s, :, at] = acc_rows[base + (1 - core) * piece_tiles + t]
    for s in range(rows):
        base = jnp.bitwise_xor(row, s) * piece_tiles
        for t in range(piece_tiles):
            at = slice(t * width, (t + 1) * width)
            piece = acc_cols[base + t]
            if s == 0:
                piece = piece + own[:, at] * diag[:, at]
            col_out[s, :, at] = piece


def image_kernel(copies, *refs):
    now, prev = refs[:2]
    image_out, sums_out = refs[-2:]
    image = refs[2][...]
    for ref in refs[3:-2]:
        image = image + ref[...]
    image_out[...] = image
    block, last = now[...], prev[...]
    vectors = image.shape[0]
    both = jnp.concatenate([block, last], axis=0)
    against = contract(image, jnp.concatenate([image, both], axis=0))
    fixed = contract(both, both)
    half = sums_out.shape[2] // 2
    used = against.shape[1] + 2 * fixed.shape[1]
    sums = jnp.concatenate(
        [
            against,
            fixed[:vectors],
            fixed[vectors:],
            jnp.zeros((vectors, half - used), jnp.float32),
        ],
        axis=1,
    )
    sums = jnp.concatenate([sums[: vectors // 2], sums[vectors // 2 :]], axis=1)
    for k in range(copies):
        sums_out[k] = sums


def finish_kernel(states, sums_in, image, now, prev, coupling, next_out, alpha_out, beta_out):
    vectors = image.shape[0]
    sums = jnp.sum(sums_in[...], axis=0) / states
    half = sums.shape[1] // 2
    sums = jnp.concatenate([sums[:, :half], sums[:, half:]], axis=0)
    image_gram = sums[:, :vectors]
    alpha_t = sums[:, vectors : 2 * vectors]
    image_prev = sums[:, 2 * vectors : 3 * vectors]
    fixed = jnp.concatenate(
        [sums[:, 3 * vectors : 5 * vectors], sums[:, 5 * vectors : 7 * vectors]], axis=0
    )
    pair = coupling[...]
    left = jnp.concatenate([alpha_t, pair], axis=1)
    seen = jnp.concatenate([alpha_t, image_prev], axis=1)
    gram = image_gram + contract(
        jnp.concatenate([matmul(left, fixed) - seen, -left], axis=1),
        jnp.concatenate([left, seen], axis=1),
    )
    row_at = lax.broadcasted_iota(jnp.int32, (vectors, vectors), 0)
    col_at = lax.broadcasted_iota(jnp.int32, (vectors, vectors), 1)
    eye = (row_at == col_at).astype(jnp.float32)
    alpha_out[...] = contract(eye, alpha_t)
    work = jnp.concatenate([gram, eye, -left], axis=1)
    below = lax.broadcasted_iota(jnp.int32, (vectors, 1), 0)
    pivots = jnp.zeros((vectors, 1), jnp.float32)
    for j in range(vectors):
        pivot = work[j : j + 1, j : j + 1]
        line = work[j : j + 1, :]
        pivots = jnp.where(below == j, pivot, pivots)
        if j + 1 < vectors:
            factor = jnp.where(below > j, work[:, j : j + 1] / pivot, 0.0)
            work = work - factor * line
    work = work / jnp.sqrt(pivots)
    beta_out[...] = jnp.where(col_at >= row_at, work[:, :vectors], 0.0)
    next_out[...] = matmul(
        work[:, vectors:], jnp.concatenate([image[...], now[...], prev[...]], axis=0)
    )


def local(rows, cols, tiles, tile_rows, tile_cols, tile_counts, block_now, block_prev, coupling, diag_energy):
    slots, width = tiles.shape[2], tiles.shape[4]
    vectors, piece = block_now.shape
    piece_tiles = piece // width
    planes = cols // 2
    f32 = jnp.float32
    piece_shape = jax.ShapeDtypeStruct((vectors, piece), f32)

    def along_col(x, s):
        return lax.ppermute(x, "col", [(i, i ^ s) for i in range(cols)])

    def along_row(x, s):
        return lax.ppermute(x, "row", [(i, i ^ s) for i in range(rows)])

    def apart(x, s):
        pairs = []
        for r in range(rows):
            for c in range(cols):
                if c % 2 == 0:
                    to = (r, c ^ (2 * s) if s < planes else c)
                else:
                    to = (r ^ s if s < rows else r, c)
                pairs.append((r * cols + c, to[0] * cols + to[1]))
        return lax.ppermute(x, ("row", "col"), pairs)

    beside = along_col(block_now, 1)
    chip = jnp.concatenate([block_now, beside], axis=0)
    peers = range(1, max(planes, rows))
    fetched = [apart(chip, s) for s in peers]
    passed = [along_col(x, 1) for x in fetched]

    in_vmem = pl.BlockSpec(memory_space=VMEM)
    in_hbm = pl.BlockSpec(memory_space=pltpu.HBM)
    group = math.gcd(slots, GROUP)

    def stay(x):
        return pltpu.with_memory_space_constraint(x, pltpu.HBM)

    keep, send, col_parts = pl.pallas_call(
        functools.partial(products_kernel, rows, planes, group),
        out_shape=(
            jax.ShapeDtypeStruct((planes, vectors, piece), f32),
            jax.ShapeDtypeStruct((planes, vectors, piece), f32),
            jax.ShapeDtypeStruct((rows, vectors, piece), f32),
        ),
        in_specs=[pl.BlockSpec(memory_space=SMEM)]
        + [in_hbm] * 5
        + [in_vmem] * (1 + 2 * len(peers)),
        out_specs=(in_vmem,) * 3,
        scratch_shapes=[
            VMEM((slots, width, width), f32),
            SMEM(tile_rows.shape, jnp.int32),
            SMEM(tile_cols.shape, jnp.int32),
            VMEM((1, piece), f32),
            VMEM((vectors, piece), f32),
            VMEM((cols * piece_tiles, 2 * vectors, width), jnp.bfloat16),
            VMEM((rows * piece_tiles, 2 * vectors, width), jnp.bfloat16),
            VMEM((cols * piece_tiles + 1, vectors, width), f32),
            VMEM((rows * piece_tiles + 1, vectors, width), f32),
            pltpu.SemaphoreType.DMA((4,)),
            pltpu.SemaphoreType.DMA((slots // group,)),
        ],
        compiler_params=pltpu.CompilerParams(vmem_limit_bytes=40 * MIB),
        name="products",
    )(
        tile_counts,
        stay(tiles.reshape(slots, width, width)),
        stay(tile_rows),
        stay(tile_cols),
        stay(diag_energy.reshape(1, piece)),
        stay(block_now),
        beside,
        *fetched,
        *passed,
    )

    back_rows = [along_row(col_parts[s], s) for s in range(1, rows)]
    from_core = along_col(send, 1)
    summed = [keep[s] + from_core[s] for s in range(1, planes)]
    back_planes = [along_col(summed[s - 1], 2 * s) for s in range(1, planes)]
    terms = [keep[0], from_core[0], col_parts[0], *back_planes, *back_rows]

    devices = rows * cols
    image, sums = pl.pallas_call(
        functools.partial(image_kernel, devices),
        out_shape=(
            piece_shape,
            jax.ShapeDtypeStruct((devices, vectors // 2, 128), f32),
        ),
        in_specs=[in_vmem] * (2 + len(terms)),
        out_specs=(in_vmem,) * 2,
        compiler_params=pltpu.CompilerParams(vmem_limit_bytes=16 * MIB),
        name="image",
    )(block_now, block_prev, *terms)

    sums = lax.all_to_all(sums, ("row", "col"), 0, 0)
    return pl.pallas_call(
        functools.partial(finish_kernel, float(piece * devices)),
        out_shape=(
            piece_shape,
            jax.ShapeDtypeStruct((vectors, vectors), f32),
            jax.ShapeDtypeStruct((vectors, vectors), f32),
        ),
        in_specs=[in_vmem] * 5,
        out_specs=(in_vmem,) * 3,
        compiler_params=pltpu.CompilerParams(vmem_limit_bytes=16 * MIB),
        name="finish",
    )(sums, image, block_now, block_prev, coupling)


def solution(mesh):
    return jax.shard_map(
        functools.partial(local, mesh.shape["row"], mesh.shape["col"]),
        mesh=mesh,
        in_specs=(
            P("row", "col", None, None, None),
            P("row", "col", None),
            P("row", "col", None),
            P("row", "col"),
            P(None, ("row", "col")),
            P(None, ("row", "col")),
            P(),
            P(("row", "col")),
        ),
        out_specs=(P(None, ("row", "col")), P(), P()),
        check_vma=False,
    )
```

```python
import functools
import math

import jax
import jax.numpy as jnp
from jax import lax
from jax.experimental import pallas as pl
from jax.experimental.pallas import tpu as pltpu
from jax.sharding import PartitionSpec as P

VMEM = pltpu.VMEM
SMEM = pltpu.SMEM
GROUP = 32
WAIT_FLOPS = 20_000_000_000
MIB = 1 << 20


def halves(x):
    high = x.astype(jnp.bfloat16)
    low = (x - high.astype(jnp.float32)).astype(jnp.bfloat16)
    return high, low


def contract(left, right):
    return lax.dot_general(
        left,
        right,
        (((1,), (1,)), ((), ())),
        precision=lax.Precision.HIGHEST,
        preferred_element_type=jnp.float32,
    )


def matmul(left, right):
    return jnp.dot(
        left, right, precision=lax.Precision.HIGHEST, preferred_element_type=jnp.float32
    )


def products_kernel(rows, planes, group, *refs):
    peers = max(planes, rows) - 1
    count, tiles, row_idx_hbm, col_idx_hbm, diag_hbm, own_hbm, beside = refs[:7]
    fetched = refs[7 : 7 + peers]
    passed = refs[7 + peers : 7 + 2 * peers]
    (
        keep_out,
        send_out,
        col_out,
        row_idx,
        col_idx,
        diag,
        own,
        vec_rows,
        vec_cols,
        acc_rows,
        acc_cols,
        small_sems,
    ) = refs[7 + 2 * peers :]
    row = lax.axis_index("row")
    col = lax.axis_index("col")
    plane, core = col // 2, col % 2
    vectors = own.shape[0]
    width = tiles.shape[-1]
    piece_tiles = own.shape[1] // width
    first = core == 0

    small = [
        pltpu.make_async_copy(source, target, small_sems.at[k])
        for k, (source, target) in enumerate(
            (
                (row_idx_hbm, row_idx),
                (col_idx_hbm, col_idx),
                (own_hbm, own),
                (diag_hbm, diag),
            )
        )
    ]

    total = count[0, 0]
    groups = (total + group - 1) // group

    for copy in small:
        copy.start()
    acc_rows[...] = jnp.zeros_like(acc_rows)
    acc_cols[...] = jnp.zeros_like(acc_cols)

    def store_split(target, base, read):
        for t in range(piece_tiles):
            high, low = halves(read(slice(t * width, (t + 1) * width)))
            target[base + t] = jnp.concatenate([high, low], axis=0)

    for s in range(1, planes):
        base = jnp.bitwise_xor(plane, s) * 2 * piece_tiles
        for side in range(2):
            part = slice(side * vectors, (side + 1) * vectors)
            store_split(
                vec_rows,
                base + side * piece_tiles,
                lambda at: jnp.where(first, fetched[s - 1][part, at], passed[s - 1][part, at]),
            )
    for s in range(1, rows):
        store_split(
            vec_cols,
            jnp.bitwise_xor(row, s) * piece_tiles,
            lambda at: jnp.where(
                first, passed[s - 1][vectors:, at], fetched[s - 1][:vectors, at]
            ),
        )
    store_split(vec_rows, (col + 1 - 2 * core) * piece_tiles, lambda at: beside[:, at])
    for copy in small:
        copy.wait()
    store_split(vec_rows, col * piece_tiles, lambda at: own[:, at])
    store_split(vec_cols, row * piece_tiles, lambda at: own[:, at])

    spare_row = acc_rows.shape[0] - 1
    spare_col = acc_cols.shape[0] - 1

    def multiply(g, carry):
        for k in range(group):
            m = g * group + k
            alive = m < total
            r, c = row_idx[0, 0, m], col_idx[0, 0, m]
            high, low = halves(tiles[m])
            from_row = vec_rows[r]
            from_col = vec_cols[c]
            back = jnp.dot(
                jnp.concatenate([from_row, from_row], axis=1),
                jnp.concatenate([high, low], axis=0),
                preferred_element_type=jnp.float32,
            )
            ahead = lax.dot_general(
                jnp.concatenate([high, low], axis=1),
                jnp.concatenate([from_col, from_col], axis=1),
                (((1,), (1,)), ((), ())),
                preferred_element_type=jnp.float32,
            ).T
            acc_rows[jnp.where(alive, r, spare_row)] += ahead[:8] + ahead[8:]
            acc_cols[jnp.where(alive, c, spare_col)] += back[:8] + back[8:]
        return carry

    lax.fori_loop(0, groups, multiply, 0)

    for s in range(planes):
        base = jnp.bitwise_xor(plane, s) * 2 * piece_tiles
        for t in range(piece_tiles):
            at = slice(t * width, (t + 1) * width)
            keep_out[s, :, at] = acc_rows[base + core * piece_tiles + t]
            send_out[s, :, at] = acc_rows[base + (1 - core) * piece_tiles + t]
    for s in range(rows):
        base = jnp.bitwise_xor(row, s) * piece_tiles
        for t in range(piece_tiles):
            at = slice(t * width, (t + 1) * width)
            piece = acc_cols[base + t]
            if s == 0:
                piece = piece + own[:, at] * diag[:, at]
            col_out[s, :, at] = piece


def fixed_kernel(now, prev, out, both, sems):
    vectors = now.shape[0]
    copies = [
        pltpu.make_async_copy(now, both.at[pl.ds(0, vectors)], sems.at[0]),
        pltpu.make_async_copy(prev, both.at[pl.ds(vectors, vectors)], sems.at[1]),
    ]
    for copy in copies:
        copy.start()
    for copy in copies:
        copy.wait()
    out[...] = contract(both[...], both[...])


def image_kernel(copies, *refs):
    now, prev, fixed_in = refs[:3]
    image_out, sums_out = refs[-2:]
    image = refs[3][...]
    for ref in refs[4:-2]:
        image = image + ref[...]
    image_out[...] = image
    block, last = now[...], prev[...]
    vectors = image.shape[0]
    both = jnp.concatenate([block, last], axis=0)
    against = contract(image, jnp.concatenate([image, both], axis=0))
    fixed = fixed_in[...]
    half = sums_out.shape[2] // 2
    used = against.shape[1] + 2 * fixed.shape[1]
    sums = jnp.concatenate(
        [
            against,
            fixed[:vectors],
            fixed[vectors:],
            jnp.zeros((vectors, half - used), jnp.float32),
        ],
        axis=1,
    )
    sums = jnp.concatenate([sums[: vectors // 2], sums[vectors // 2 :]], axis=1)
    for k in range(copies):
        sums_out[k] = sums


def finish_kernel(states, sums_in, image, now, prev, coupling, next_out, alpha_out, beta_out):
    vectors = image.shape[0]
    sums = jnp.sum(sums_in[...], axis=0) / states
    half = sums.shape[1] // 2
    sums = jnp.concatenate([sums[:, :half], sums[:, half:]], axis=0)
    image_gram = sums[:, :vectors]
    alpha_t = sums[:, vectors : 2 * vectors]
    image_prev = sums[:, 2 * vectors : 3 * vectors]
    fixed = jnp.concatenate(
        [sums[:, 3 * vectors : 5 * vectors], sums[:, 5 * vectors : 7 * vectors]], axis=0
    )
    pair = coupling[...]
    left = jnp.concatenate([alpha_t, pair], axis=1)
    seen = jnp.concatenate([alpha_t, image_prev], axis=1)
    gram = image_gram + contract(
        jnp.concatenate([matmul(left, fixed) - seen, -left], axis=1),
        jnp.concatenate([left, seen], axis=1),
    )
    row_at = lax.broadcasted_iota(jnp.int32, (vectors, vectors), 0)
    col_at = lax.broadcasted_iota(jnp.int32, (vectors, vectors), 1)
    eye = (row_at == col_at).astype(jnp.float32)
    alpha_out[...] = contract(eye, alpha_t)
    work = jnp.concatenate([gram, eye, -left], axis=1)
    below = lax.broadcasted_iota(jnp.int32, (vectors, 1), 0)
    pivots = jnp.zeros((vectors, 1), jnp.float32)
    for j in range(vectors):
        pivot = work[j : j + 1, j : j + 1]
        line = work[j : j + 1, :]
        pivots = jnp.where(below == j, pivot, pivots)
        if j + 1 < vectors:
            factor = jnp.where(below > j, work[:, j : j + 1] / pivot, 0.0)
            work = work - factor * line
    work = work / jnp.sqrt(pivots)
    beta_out[...] = jnp.where(col_at >= row_at, work[:, :vectors], 0.0)
    next_out[...] = matmul(
        work[:, vectors:], jnp.concatenate([image[...], now[...], prev[...]], axis=0)
    )


def local(rows, cols, tiles, tile_rows, tile_cols, tile_counts, block_now, block_prev, coupling, diag_energy):
    slots, width = tiles.shape[2], tiles.shape[4]
    vectors, piece = block_now.shape
    piece_tiles = piece // width
    planes = cols // 2
    f32 = jnp.float32
    piece_shape = jax.ShapeDtypeStruct((vectors, piece), f32)

    def along_col(x, s):
        return lax.ppermute(x, "col", [(i, i ^ s) for i in range(cols)])

    def along_row(x, s):
        return lax.ppermute(x, "row", [(i, i ^ s) for i in range(rows)])

    def apart(x, s):
        pairs = []
        for r in range(rows):
            for c in range(cols):
                if c % 2 == 0:
                    to = (r, c ^ (2 * s) if s < planes else c)
                else:
                    to = (r ^ s if s < rows else r, c)
                pairs.append((r * cols + c, to[0] * cols + to[1]))
        return lax.ppermute(x, ("row", "col"), pairs)

    in_vmem = pl.BlockSpec(memory_space=VMEM)
    in_hbm = pl.BlockSpec(memory_space=pltpu.HBM)

    def stay(x):
        return pltpu.with_memory_space_constraint(x, pltpu.HBM)

    fixed = pl.pallas_call(
        fixed_kernel,
        out_shape=jax.ShapeDtypeStruct((2 * vectors, 2 * vectors), f32),
        in_specs=[in_hbm] * 2,
        out_specs=in_vmem,
        scratch_shapes=[
            VMEM((2 * vectors, piece), f32),
            pltpu.SemaphoreType.DMA((2,)),
        ],
        compiler_params=pltpu.CompilerParams(vmem_limit_bytes=16 * MIB),
        cost_estimate=pl.CostEstimate(
            flops=WAIT_FLOPS, bytes_accessed=2 * vectors * piece * 4, transcendentals=0
        ),
        name="fixed",
    )(stay(block_now), stay(block_prev))
    beside = along_col(block_now, 1)
    chip = jnp.concatenate([block_now, beside], axis=0)
    peers = range(1, max(planes, rows))
    fetched = [apart(chip, s) for s in peers]
    fetched[-1], fixed = lax.optimization_barrier((fetched[-1], fixed))
    passed = [along_col(x, 1) for x in fetched]

    group = math.gcd(slots, GROUP)

    keep, send, col_parts = pl.pallas_call(
        functools.partial(products_kernel, rows, planes, group),
        out_shape=(
            jax.ShapeDtypeStruct((planes, vectors, piece), f32),
            jax.ShapeDtypeStruct((planes, vectors, piece), f32),
            jax.ShapeDtypeStruct((rows, vectors, piece), f32),
        ),
        in_specs=[pl.BlockSpec(memory_space=SMEM)]
        + [in_vmem]
        + [in_hbm] * 4
        + [in_vmem] * (1 + 2 * len(peers)),
        out_specs=(in_vmem,) * 3,
        scratch_shapes=[
            SMEM(tile_rows.shape, jnp.int32),
            SMEM(tile_cols.shape, jnp.int32),
            VMEM((1, piece), f32),
            VMEM((vectors, piece), f32),
            VMEM((cols * piece_tiles, 2 * vectors, width), jnp.bfloat16),
            VMEM((rows * piece_tiles, 2 * vectors, width), jnp.bfloat16),
            VMEM((cols * piece_tiles + 1, vectors, width), f32),
            VMEM((rows * piece_tiles + 1, vectors, width), f32),
            pltpu.SemaphoreType.DMA((4,)),
        ],
        compiler_params=pltpu.CompilerParams(vmem_limit_bytes=20 * MIB),
        name="products",
    )(
        tile_counts,
        pltpu.with_memory_space_constraint(tiles.reshape(slots, width, width), VMEM),
        stay(tile_rows),
        stay(tile_cols),
        stay(diag_energy.reshape(1, piece)),
        stay(block_now),
        beside,
        *fetched,
        *passed,
    )

    back_rows = [along_row(col_parts[s], s) for s in range(1, rows)]
    from_core = along_col(send, 1)
    summed = [keep[s] + from_core[s] for s in range(1, planes)]
    back_planes = [along_col(summed[s - 1], 2 * s) for s in range(1, planes)]
    terms = [keep[0], from_core[0], col_parts[0], *back_planes, *back_rows]

    devices = rows * cols
    image, sums = pl.pallas_call(
        functools.partial(image_kernel, devices),
        out_shape=(
            piece_shape,
            jax.ShapeDtypeStruct((devices, vectors // 2, 128), f32),
        ),
        in_specs=[in_vmem] * (3 + len(terms)),
        out_specs=(in_vmem,) * 2,
        compiler_params=pltpu.CompilerParams(vmem_limit_bytes=16 * MIB),
        name="image",
    )(block_now, block_prev, fixed, *terms)

    sums = lax.all_to_all(sums, ("row", "col"), 0, 0)
    return pl.pallas_call(
        functools.partial(finish_kernel, float(piece * devices)),
        out_shape=(
            piece_shape,
            jax.ShapeDtypeStruct((vectors, vectors), f32),
            jax.ShapeDtypeStruct((vectors, vectors), f32),
        ),
        in_specs=[in_vmem] * 5,
        out_specs=(in_vmem,) * 3,
        compiler_params=pltpu.CompilerParams(vmem_limit_bytes=16 * MIB),
        name="finish",
    )(sums, image, block_now, block_prev, coupling)


def solution(mesh):
    return jax.shard_map(
        functools.partial(local, mesh.shape["row"], mesh.shape["col"]),
        mesh=mesh,
        in_specs=(
            P("row", "col", None, None, None),
            P("row", "col", None),
            P("row", "col", None),
            P("row", "col"),
            P(None, ("row", "col")),
            P(None, ("row", "col")),
            P(),
            P(("row", "col")),
        ),
        out_specs=(P(None, ("row", "col")), P(), P()),
        check_vma=False,
    )
```

```python
import functools
import math

import jax
import jax.numpy as jnp
from jax import lax
from jax.experimental import pallas as pl
from jax.experimental.pallas import tpu as pltpu
from jax.sharding import PartitionSpec as P

VMEM = pltpu.VMEM
SMEM = pltpu.SMEM
GROUP = 64
WAIT_FLOPS = 20_000_000_000
MIB = 1 << 20


def halves(x):
    high = x.astype(jnp.bfloat16)
    low = (x - high.astype(jnp.float32)).astype(jnp.bfloat16)
    return high, low


def contract(left, right):
    return lax.dot_general(
        left,
        right,
        (((1,), (1,)), ((), ())),
        precision=lax.Precision.HIGHEST,
        preferred_element_type=jnp.float32,
    )


def matmul(left, right):
    return jnp.dot(
        left, right, precision=lax.Precision.HIGHEST, preferred_element_type=jnp.float32
    )


def products_kernel(rows, planes, group, *refs):
    peers = max(planes, rows) - 1
    count, tiles, row_idx_hbm, col_idx_hbm, diag_hbm, chip = refs[:6]
    fetched = refs[6 : 6 + peers]
    passed = refs[6 + peers : 6 + 2 * peers]
    (
        keep_out,
        send_out,
        col_out,
        row_idx,
        col_idx,
        diag,
        vec_rows,
        vec_cols,
        acc_rows,
        acc_cols,
        small_sems,
    ) = refs[6 + 2 * peers :]
    row = lax.axis_index("row")
    col = lax.axis_index("col")
    plane, core = col // 2, col % 2
    vectors = chip.shape[0] // 2
    width = tiles.shape[-1]
    piece_tiles = chip.shape[1] // width
    first = core == 0

    small = [
        pltpu.make_async_copy(source, target, small_sems.at[k])
        for k, (source, target) in enumerate(
            (
                (row_idx_hbm, row_idx),
                (col_idx_hbm, col_idx),
                (diag_hbm, diag),
            )
        )
    ]

    total = count[0, 0]
    groups = (total + group - 1) // group

    for copy in small:
        copy.start()
    acc_rows[...] = jnp.zeros_like(acc_rows)
    acc_cols[...] = jnp.zeros_like(acc_cols)

    def store_split(target, base, read):
        for t in range(piece_tiles):
            high, low = halves(read(slice(t * width, (t + 1) * width)))
            target[base + t] = jnp.concatenate([high, low], axis=0)

    for s in range(1, planes):
        base = jnp.bitwise_xor(plane, s) * 2 * piece_tiles
        for side in range(2):
            part = slice(side * vectors, (side + 1) * vectors)
            store_split(
                vec_rows,
                base + side * piece_tiles,
                lambda at: jnp.where(first, fetched[s - 1][part, at], passed[s - 1][part, at]),
            )
    for s in range(1, rows):
        store_split(
            vec_cols,
            jnp.bitwise_xor(row, s) * piece_tiles,
            lambda at: jnp.where(
                first, passed[s - 1][vectors:, at], fetched[s - 1][:vectors, at]
            ),
        )
    store_split(vec_rows, col * piece_tiles, lambda at: chip[:vectors, at])
    store_split(vec_rows, (col + 1 - 2 * core) * piece_tiles, lambda at: chip[vectors:, at])
    store_split(vec_cols, row * piece_tiles, lambda at: chip[:vectors, at])
    small[0].wait()
    small[1].wait()

    spare_row = acc_rows.shape[0] - 1
    spare_col = acc_cols.shape[0] - 1

    def multiply(g, carry):
        for k in range(group):
            m = g * group + k
            alive = m < total
            r, c = row_idx[0, 0, m], col_idx[0, 0, m]
            high, low = halves(tiles[m])
            from_row = vec_rows[r]
            from_col = vec_cols[c]
            back = jnp.dot(
                jnp.concatenate([from_row, from_row], axis=1),
                jnp.concatenate([high, low], axis=0),
                preferred_element_type=jnp.float32,
            )
            ahead = lax.dot_general(
                jnp.concatenate([high, low], axis=1),
                jnp.concatenate([from_col, from_col], axis=1),
                (((1,), (1,)), ((), ())),
                preferred_element_type=jnp.float32,
            ).T
            acc_rows[jnp.where(alive, r, spare_row)] += ahead[:8] + ahead[8:]
            acc_cols[jnp.where(alive, c, spare_col)] += back[:8] + back[8:]
        return carry

    lax.fori_loop(0, groups, multiply, 0)
    small[2].wait()

    for s in range(planes):
        base = jnp.bitwise_xor(plane, s) * 2 * piece_tiles
        for t in range(piece_tiles):
            at = slice(t * width, (t + 1) * width)
            keep_out[s, :, at] = acc_rows[base + core * piece_tiles + t]
            send_out[s, :, at] = acc_rows[base + (1 - core) * piece_tiles + t]
    for s in range(rows):
        base = jnp.bitwise_xor(row, s) * piece_tiles
        for t in range(piece_tiles):
            at = slice(t * width, (t + 1) * width)
            piece = acc_cols[base + t]
            if s == 0:
                piece = piece + chip[:vectors, at] * diag[:, at]
            col_out[s, :, at] = piece


def fixed_kernel(now, prev, out, both, sems):
    vectors = now.shape[0]
    copies = [
        pltpu.make_async_copy(now, both.at[pl.ds(0, vectors)], sems.at[0]),
        pltpu.make_async_copy(prev, both.at[pl.ds(vectors, vectors)], sems.at[1]),
    ]
    for copy in copies:
        copy.start()
    for copy in copies:
        copy.wait()
    out[...] = contract(both[...], both[...])


def image_kernel(copies, *refs):
    now, prev, fixed_in = refs[:3]
    image_out, sums_out = refs[-2:]
    image = refs[3][...]
    for ref in refs[4:-2]:
        image = image + ref[...]
    image_out[...] = image
    block, last = now[...], prev[...]
    vectors = image.shape[0]
    both = jnp.concatenate([block, last], axis=0)
    against = contract(image, jnp.concatenate([image, both], axis=0))
    fixed = fixed_in[...]
    half = sums_out.shape[2] // 2
    used = against.shape[1] + 2 * fixed.shape[1]
    sums = jnp.concatenate(
        [
            against,
            fixed[:vectors],
            fixed[vectors:],
            jnp.zeros((vectors, half - used), jnp.float32),
        ],
        axis=1,
    )
    sums = jnp.concatenate([sums[: vectors // 2], sums[vectors // 2 :]], axis=1)
    for k in range(copies):
        sums_out[k] = sums


def finish_kernel(states, sums_in, image, now, prev, coupling, next_out, alpha_out, beta_out):
    vectors = image.shape[0]
    sums = jnp.sum(sums_in[...], axis=0) / states
    half = sums.shape[1] // 2
    sums = jnp.concatenate([sums[:, :half], sums[:, half:]], axis=0)
    image_gram = sums[:, :vectors]
    alpha_t = sums[:, vectors : 2 * vectors]
    image_prev = sums[:, 2 * vectors : 3 * vectors]
    fixed = jnp.concatenate(
        [sums[:, 3 * vectors : 5 * vectors], sums[:, 5 * vectors : 7 * vectors]], axis=0
    )
    pair = coupling[...]
    left = jnp.concatenate([alpha_t, pair], axis=1)
    seen = jnp.concatenate([alpha_t, image_prev], axis=1)
    gram = image_gram + contract(
        jnp.concatenate([matmul(left, fixed) - seen, -left], axis=1),
        jnp.concatenate([left, seen], axis=1),
    )
    row_at = lax.broadcasted_iota(jnp.int32, (vectors, vectors), 0)
    col_at = lax.broadcasted_iota(jnp.int32, (vectors, vectors), 1)
    eye = (row_at == col_at).astype(jnp.float32)
    alpha_out[...] = contract(eye, alpha_t)
    work = jnp.concatenate([gram, eye, -left], axis=1)
    line_at = lax.broadcasted_iota(jnp.int32, work.shape, 0)
    pivots = jnp.ones_like(work)
    for j in range(vectors):
        column = jnp.broadcast_to(work[:, j : j + 1], work.shape)
        line = jnp.broadcast_to(work[j : j + 1, :], work.shape)
        pivot = jnp.broadcast_to(column[j : j + 1, :], work.shape)
        pivots = jnp.where(line_at == j, pivot, pivots)
        work = work - jnp.where(line_at > j, column, 0.0) * (line / pivot)
    work = work / jnp.sqrt(pivots)
    beta_out[...] = jnp.where(col_at >= row_at, work[:, :vectors], 0.0)
    next_out[...] = matmul(
        work[:, vectors:], jnp.concatenate([image[...], now[...], prev[...]], axis=0)
    )


def local(rows, cols, tiles, tile_rows, tile_cols, tile_counts, block_now, block_prev, coupling, diag_energy):
    slots, width = tiles.shape[2], tiles.shape[4]
    vectors, piece = block_now.shape
    piece_tiles = piece // width
    planes = cols // 2
    f32 = jnp.float32
    piece_shape = jax.ShapeDtypeStruct((vectors, piece), f32)

    def along_col(x, s):
        return lax.ppermute(x, "col", [(i, i ^ s) for i in range(cols)])

    def along_row(x, s):
        return lax.ppermute(x, "row", [(i, i ^ s) for i in range(rows)])

    def apart(x, s):
        pairs = []
        for r in range(rows):
            for c in range(cols):
                if c % 2 == 0:
                    to = (r, c ^ (2 * s) if s < planes else c)
                else:
                    to = (r ^ s if s < rows else r, c)
                pairs.append((r * cols + c, to[0] * cols + to[1]))
        return lax.ppermute(x, ("row", "col"), pairs)

    in_vmem = pl.BlockSpec(memory_space=VMEM)
    in_hbm = pl.BlockSpec(memory_space=pltpu.HBM)

    def stay(x):
        return pltpu.with_memory_space_constraint(x, pltpu.HBM)

    fixed = pl.pallas_call(
        fixed_kernel,
        out_shape=jax.ShapeDtypeStruct((2 * vectors, 2 * vectors), f32),
        in_specs=[in_hbm] * 2,
        out_specs=in_vmem,
        scratch_shapes=[
            VMEM((2 * vectors, piece), f32),
            pltpu.SemaphoreType.DMA((2,)),
        ],
        compiler_params=pltpu.CompilerParams(vmem_limit_bytes=16 * MIB),
        cost_estimate=pl.CostEstimate(
            flops=WAIT_FLOPS, bytes_accessed=2 * vectors * piece * 4, transcendentals=0
        ),
        name="fixed",
    )(stay(block_now), stay(block_prev))
    beside = along_col(block_now, 1)
    chip = jnp.concatenate([block_now, beside], axis=0)
    peers = range(1, max(planes, rows))
    fetched = [apart(chip, s) for s in peers]
    fetched[0], fixed = lax.optimization_barrier((fetched[0], fixed))
    passed = [along_col(x, 1) for x in fetched]

    group = math.gcd(slots, GROUP)

    keep, send, col_parts = pl.pallas_call(
        functools.partial(products_kernel, rows, planes, group),
        out_shape=(
            jax.ShapeDtypeStruct((planes, vectors, piece), f32),
            jax.ShapeDtypeStruct((planes, vectors, piece), f32),
            jax.ShapeDtypeStruct((rows, vectors, piece), f32),
        ),
        in_specs=[pl.BlockSpec(memory_space=SMEM)]
        + [in_vmem]
        + [in_hbm] * 3
        + [in_vmem] * (1 + 2 * len(peers)),
        out_specs=(in_vmem,) * 3,
        scratch_shapes=[
            SMEM(tile_rows.shape, jnp.int32),
            SMEM(tile_cols.shape, jnp.int32),
            VMEM((1, piece), f32),
            VMEM((cols * piece_tiles, 2 * vectors, width), jnp.bfloat16),
            VMEM((rows * piece_tiles, 2 * vectors, width), jnp.bfloat16),
            VMEM((cols * piece_tiles + 1, vectors, width), f32),
            VMEM((rows * piece_tiles + 1, vectors, width), f32),
            pltpu.SemaphoreType.DMA((3,)),
        ],
        compiler_params=pltpu.CompilerParams(vmem_limit_bytes=20 * MIB),
        name="products",
    )(
        tile_counts,
        pltpu.with_memory_space_constraint(tiles.reshape(slots, width, width), VMEM),
        stay(tile_rows),
        stay(tile_cols),
        stay(diag_energy.reshape(1, piece)),
        chip,
        *fetched,
        *passed,
    )

    back_rows = [along_row(col_parts[s], s) for s in range(1, rows)]
    from_core = along_col(send, 1)
    summed = [keep[s] + from_core[s] for s in range(1, planes)]
    back_planes = [along_col(summed[s - 1], 2 * s) for s in range(1, planes)]
    terms = [keep[0], from_core[0], col_parts[0], *back_planes, *back_rows]

    devices = rows * cols
    image, sums = pl.pallas_call(
        functools.partial(image_kernel, devices),
        out_shape=(
            piece_shape,
            jax.ShapeDtypeStruct((devices, vectors // 2, 128), f32),
        ),
        in_specs=[in_vmem] * (3 + len(terms)),
        out_specs=(in_vmem,) * 2,
        compiler_params=pltpu.CompilerParams(vmem_limit_bytes=16 * MIB),
        name="image",
    )(block_now, block_prev, fixed, *terms)

    sums = lax.all_to_all(sums, ("row", "col"), 0, 0)
    return pl.pallas_call(
        functools.partial(finish_kernel, float(piece * devices)),
        out_shape=(
            piece_shape,
            jax.ShapeDtypeStruct((vectors, vectors), f32),
            jax.ShapeDtypeStruct((vectors, vectors), f32),
        ),
        in_specs=[in_vmem] * 5,
        out_specs=(in_vmem,) * 3,
        compiler_params=pltpu.CompilerParams(vmem_limit_bytes=16 * MIB),
        name="finish",
    )(sums, image, block_now, block_prev, coupling)


def solution(mesh):
    return jax.shard_map(
        functools.partial(local, mesh.shape["row"], mesh.shape["col"]),
        mesh=mesh,
        in_specs=(
            P("row", "col", None, None, None),
            P("row", "col", None),
            P("row", "col", None),
            P("row", "col"),
            P(None, ("row", "col")),
            P(None, ("row", "col")),
            P(),
            P(("row", "col")),
        ),
        out_specs=(P(None, ("row", "col")), P(), P()),
        check_vma=False,
    )
```

```python
import functools
import math

import jax
import jax.numpy as jnp
from jax import lax
from jax.experimental import pallas as pl
from jax.experimental.pallas import tpu as pltpu
from jax.sharding import PartitionSpec as P

VMEM = pltpu.VMEM
SMEM = pltpu.SMEM
GROUP = 64
WAIT_FLOPS = 20_000_000_000
MIB = 1 << 20


def halves(x):
    high = x.astype(jnp.bfloat16)
    low = (x - high.astype(jnp.float32)).astype(jnp.bfloat16)
    return high, low


def contract(left, right):
    return lax.dot_general(
        left,
        right,
        (((1,), (1,)), ((), ())),
        precision=lax.Precision.HIGHEST,
        preferred_element_type=jnp.float32,
    )


def matmul(left, right):
    return jnp.dot(
        left, right, precision=lax.Precision.HIGHEST, preferred_element_type=jnp.float32
    )


def products_kernel(rows, planes, group, *refs):
    peers = max(planes, rows) - 1
    count, tiles, row_idx_hbm, col_idx_hbm, diag_hbm, chip = refs[:6]
    fetched = refs[6 : 6 + peers]
    passed = refs[6 + peers : 6 + 2 * peers]
    (
        keep_out,
        send_out,
        col_out,
        row_idx,
        col_idx,
        diag,
        vec_rows,
        vec_cols,
        acc_rows,
        acc_cols,
        small_sems,
    ) = refs[6 + 2 * peers :]
    row = lax.axis_index("row")
    col = lax.axis_index("col")
    plane, core = col // 2, col % 2
    vectors = chip.shape[0] // 2
    width = tiles.shape[-1]
    piece_tiles = chip.shape[1] // width
    first = core == 0

    small = [
        pltpu.make_async_copy(source, target, small_sems.at[k])
        for k, (source, target) in enumerate(
            (
                (row_idx_hbm, row_idx),
                (col_idx_hbm, col_idx),
                (diag_hbm, diag),
            )
        )
    ]

    total = count[0, 0]
    groups = (total + group - 1) // group

    for copy in small:
        copy.start()
    acc_rows[...] = jnp.zeros_like(acc_rows)
    acc_cols[...] = jnp.zeros_like(acc_cols)

    def store_split(target, base, read):
        for t in range(piece_tiles):
            high, low = halves(read(slice(t * width, (t + 1) * width)))
            target[base + t] = jnp.concatenate([high, low], axis=0)

    for s in range(1, planes):
        base = jnp.bitwise_xor(plane, s) * 2 * piece_tiles
        for side in range(2):
            part = slice(side * vectors, (side + 1) * vectors)
            store_split(
                vec_rows,
                base + side * piece_tiles,
                lambda at: jnp.where(first, fetched[s - 1][part, at], passed[s - 1][part, at]),
            )
    for s in range(1, rows):
        store_split(
            vec_cols,
            jnp.bitwise_xor(row, s) * piece_tiles,
            lambda at: jnp.where(
                first, passed[s - 1][vectors:, at], fetched[s - 1][:vectors, at]
            ),
        )
    store_split(vec_rows, col * piece_tiles, lambda at: chip[:vectors, at])
    store_split(vec_rows, (col + 1 - 2 * core) * piece_tiles, lambda at: chip[vectors:, at])
    store_split(vec_cols, row * piece_tiles, lambda at: chip[:vectors, at])
    small[0].wait()
    small[1].wait()

    spare_row = acc_rows.shape[0] - 1
    spare_col = acc_cols.shape[0] - 1

    def multiply(g, carry):
        for k in range(group):
            m = g * group + k
            alive = m < total
            r, c = row_idx[0, 0, m], col_idx[0, 0, m]
            high, low = halves(tiles[m])
            from_row = vec_rows[r]
            from_col = vec_cols[c]
            back = jnp.dot(
                jnp.concatenate([from_row, from_row], axis=1),
                jnp.concatenate([high, low], axis=0),
                preferred_element_type=jnp.float32,
            )
            ahead = lax.dot_general(
                jnp.concatenate([high, low], axis=1),
                jnp.concatenate([from_col, from_col], axis=1),
                (((1,), (1,)), ((), ())),
                preferred_element_type=jnp.float32,
            ).T
            acc_rows[jnp.where(alive, r, spare_row)] += ahead[:8] + ahead[8:]
            acc_cols[jnp.where(alive, c, spare_col)] += back[:8] + back[8:]
        return carry

    lax.fori_loop(0, groups, multiply, 0)
    small[2].wait()

    for s in range(planes):
        base = jnp.bitwise_xor(plane, s) * 2 * piece_tiles
        for t in range(piece_tiles):
            at = slice(t * width, (t + 1) * width)
            keep_out[s, :, at] = acc_rows[base + core * piece_tiles + t]
            send_out[s, :, at] = acc_rows[base + (1 - core) * piece_tiles + t]
    for s in range(rows):
        base = jnp.bitwise_xor(row, s) * piece_tiles
        for t in range(piece_tiles):
            at = slice(t * width, (t + 1) * width)
            piece = acc_cols[base + t]
            if s == 0:
                piece = piece + chip[:vectors, at] * diag[:, at]
            col_out[s, :, at] = piece


def fixed_kernel(now, prev, out, both, sems):
    vectors = now.shape[0]
    copies = [
        pltpu.make_async_copy(now, both.at[pl.ds(0, vectors)], sems.at[0]),
        pltpu.make_async_copy(prev, both.at[pl.ds(vectors, vectors)], sems.at[1]),
    ]
    for copy in copies:
        copy.start()
    for copy in copies:
        copy.wait()
    out[...] = contract(both[...], both[...])


def image_kernel(copies, *refs):
    now, prev, fixed_in = refs[:3]
    image_out, sums_out = refs[-2:]
    image = refs[3][...]
    for ref in refs[4:-2]:
        image = image + ref[...]
    image_out[...] = image
    block, last = now[...], prev[...]
    vectors = image.shape[0]
    both = jnp.concatenate([block, last], axis=0)
    against = contract(image, jnp.concatenate([image, both], axis=0))
    fixed = fixed_in[...]
    half = sums_out.shape[2] // 2
    used = against.shape[1] + 2 * fixed.shape[1]
    sums = jnp.concatenate(
        [
            against,
            fixed[:vectors],
            fixed[vectors:],
            jnp.zeros((vectors, half - used), jnp.float32),
        ],
        axis=1,
    )
    sums = jnp.concatenate([sums[: vectors // 2], sums[vectors // 2 :]], axis=1)
    for k in range(copies):
        sums_out[k] = sums


def finish_kernel(states, sums_in, image, now, prev, coupling, next_out, alpha_out, beta_out):
    vectors = image.shape[0]
    sums = jnp.sum(sums_in[...], axis=0) / states
    half = sums.shape[1] // 2
    sums = jnp.concatenate([sums[:, :half], sums[:, half:]], axis=0)
    image_gram = sums[:, :vectors]
    alpha_t = sums[:, vectors : 2 * vectors]
    image_prev = sums[:, 2 * vectors : 3 * vectors]
    fixed = jnp.concatenate(
        [sums[:, 3 * vectors : 5 * vectors], sums[:, 5 * vectors : 7 * vectors]], axis=0
    )
    pair = coupling[...]
    left = jnp.concatenate([alpha_t, pair], axis=1)
    seen = jnp.concatenate([alpha_t, image_prev], axis=1)
    gram = image_gram + contract(
        jnp.concatenate([matmul(left, fixed) - seen, -left], axis=1),
        jnp.concatenate([left, seen], axis=1),
    )
    row_at = lax.broadcasted_iota(jnp.int32, (vectors, vectors), 0)
    col_at = lax.broadcasted_iota(jnp.int32, (vectors, vectors), 1)
    eye = (row_at == col_at).astype(jnp.float32)
    alpha_out[...] = contract(eye, alpha_t)
    work = jnp.concatenate([gram, eye, -left], axis=1)
    below = lax.broadcasted_iota(jnp.int32, (vectors, 1), 0)
    pivots = jnp.zeros((vectors, 1), jnp.float32)
    for j in range(vectors):
        pivot = work[j : j + 1, j : j + 1]
        line = work[j : j + 1, :]
        pivots = jnp.where(below == j, pivot, pivots)
        if j + 1 < vectors:
            factor = jnp.where(below > j, work[:, j : j + 1] / pivot, 0.0)
            work = work - factor * line
    work = work / jnp.sqrt(pivots)
    beta_out[...] = jnp.where(col_at >= row_at, work[:, :vectors], 0.0)
    next_out[...] = matmul(
        work[:, vectors:], jnp.concatenate([image[...], now[...], prev[...]], axis=0)
    )


def local(rows, cols, tiles, tile_rows, tile_cols, tile_counts, block_now, block_prev, coupling, diag_energy):
    slots, width = tiles.shape[2], tiles.shape[4]
    vectors, piece = block_now.shape
    piece_tiles = piece // width
    planes = cols // 2
    f32 = jnp.float32
    piece_shape = jax.ShapeDtypeStruct((vectors, piece), f32)

    def along_col(x, s):
        return lax.ppermute(x, "col", [(i, i ^ s) for i in range(cols)])

    def along_row(x, s):
        return lax.ppermute(x, "row", [(i, i ^ s) for i in range(rows)])

    def apart(x, s):
        pairs = []
        for r in range(rows):
            for c in range(cols):
                if c % 2 == 0:
                    to = (r, c ^ (2 * s) if s < planes else c)
                else:
                    to = (r ^ s if s < rows else r, c)
                pairs.append((r * cols + c, to[0] * cols + to[1]))
        return lax.ppermute(x, ("row", "col"), pairs)

    in_vmem = pl.BlockSpec(memory_space=VMEM)
    in_hbm = pl.BlockSpec(memory_space=pltpu.HBM)

    def stay(x):
        return pltpu.with_memory_space_constraint(x, pltpu.HBM)

    fixed = pl.pallas_call(
        fixed_kernel,
        out_shape=jax.ShapeDtypeStruct((2 * vectors, 2 * vectors), f32),
        in_specs=[in_hbm] * 2,
        out_specs=in_vmem,
        scratch_shapes=[
            VMEM((2 * vectors, piece), f32),
            pltpu.SemaphoreType.DMA((2,)),
        ],
        compiler_params=pltpu.CompilerParams(vmem_limit_bytes=16 * MIB),
        cost_estimate=pl.CostEstimate(
            flops=WAIT_FLOPS, bytes_accessed=2 * vectors * piece * 4, transcendentals=0
        ),
        name="fixed",
    )(stay(block_now), stay(block_prev))
    beside = along_col(block_now, 1)
    chip = jnp.concatenate([block_now, beside], axis=0)
    peers = range(1, max(planes, rows))
    fetched = [apart(chip, s) for s in peers]
    fetched[0], fixed = lax.optimization_barrier((fetched[0], fixed))
    passed = [along_col(x, 1) for x in fetched]

    group = math.gcd(slots, GROUP)

    keep, send, col_parts = pl.pallas_call(
        functools.partial(products_kernel, rows, planes, group),
        out_shape=(
            jax.ShapeDtypeStruct((planes, vectors, piece), f32),
            jax.ShapeDtypeStruct((planes, vectors, piece), f32),
            jax.ShapeDtypeStruct((rows, vectors, piece), f32),
        ),
        in_specs=[pl.BlockSpec(memory_space=SMEM)]
        + [in_vmem]
        + [in_hbm] * 3
        + [in_vmem] * (1 + 2 * len(peers)),
        out_specs=(in_vmem,) * 3,
        scratch_shapes=[
            SMEM(tile_rows.shape, jnp.int32),
            SMEM(tile_cols.shape, jnp.int32),
            VMEM((1, piece), f32),
            VMEM((cols * piece_tiles, 2 * vectors, width), jnp.bfloat16),
            VMEM((rows * piece_tiles, 2 * vectors, width), jnp.bfloat16),
            VMEM((cols * piece_tiles + 1, vectors, width), f32),
            VMEM((rows * piece_tiles + 1, vectors, width), f32),
            pltpu.SemaphoreType.DMA((3,)),
        ],
        compiler_params=pltpu.CompilerParams(vmem_limit_bytes=20 * MIB),
        name="products",
    )(
        tile_counts,
        pltpu.with_memory_space_constraint(tiles.reshape(slots, width, width), VMEM),
        stay(tile_rows),
        stay(tile_cols),
        stay(diag_energy.reshape(1, piece)),
        chip,
        *fetched,
        *passed,
    )

    from_core = along_col(send, 1)
    summed = [keep[s] + from_core[s] for s in range(1, planes)]
    nearest, *summed = lax.optimization_barrier((col_parts[1], *summed))
    back_rows = [along_row(nearest, 1)]
    back_rows += [along_row(col_parts[s], s) for s in range(2, rows)]
    back_planes = [along_col(summed[s - 1], 2 * s) for s in range(1, planes)]
    terms = [keep[0], from_core[0], col_parts[0], *back_planes, *back_rows]

    devices = rows * cols
    image, sums = pl.pallas_call(
        functools.partial(image_kernel, devices),
        out_shape=(
            piece_shape,
            jax.ShapeDtypeStruct((devices, vectors // 2, 128), f32),
        ),
        in_specs=[in_vmem] * (3 + len(terms)),
        out_specs=(in_vmem,) * 2,
        compiler_params=pltpu.CompilerParams(vmem_limit_bytes=16 * MIB),
        name="image",
    )(block_now, block_prev, fixed, *terms)

    sums = lax.all_to_all(sums, ("row", "col"), 0, 0)
    return pl.pallas_call(
        functools.partial(finish_kernel, float(piece * devices)),
        out_shape=(
            piece_shape,
            jax.ShapeDtypeStruct((vectors, vectors), f32),
            jax.ShapeDtypeStruct((vectors, vectors), f32),
        ),
        in_specs=[in_vmem] * 5,
        out_specs=(in_vmem,) * 3,
        compiler_params=pltpu.CompilerParams(vmem_limit_bytes=16 * MIB),
        name="finish",
    )(sums, image, block_now, block_prev, coupling)


def solution(mesh):
    return jax.shard_map(
        functools.partial(local, mesh.shape["row"], mesh.shape["col"]),
        mesh=mesh,
        in_specs=(
            P("row", "col", None, None, None),
            P("row", "col", None),
            P("row", "col", None),
            P("row", "col"),
            P(None, ("row", "col")),
            P(None, ("row", "col")),
            P(),
            P(("row", "col")),
        ),
        out_specs=(P(None, ("row", "col")), P(), P()),
        check_vma=False,
    )
```

```python
import functools
import math

import jax
import jax.numpy as jnp
from jax import lax
from jax.experimental import pallas as pl
from jax.experimental.pallas import tpu as pltpu
from jax.sharding import PartitionSpec as P

VMEM = pltpu.VMEM
SMEM = pltpu.SMEM
GROUP = 64
WAIT_FLOPS = 20_000_000_000
MIB = 1 << 20


def halves(x):
    high = x.astype(jnp.bfloat16)
    low = (x - high.astype(jnp.float32)).astype(jnp.bfloat16)
    return high, low


def contract(left, right):
    return lax.dot_general(
        left,
        right,
        (((1,), (1,)), ((), ())),
        precision=lax.Precision.HIGHEST,
        preferred_element_type=jnp.float32,
    )


def matmul(left, right):
    return jnp.dot(
        left, right, precision=lax.Precision.HIGHEST, preferred_element_type=jnp.float32
    )


def products_kernel(rows, planes, group, *refs):
    peers = max(planes, rows) - 1
    count, tiles, row_idx_hbm, col_idx_hbm, diag_hbm, chip = refs[:6]
    fetched = refs[6 : 6 + peers]
    passed = refs[6 + peers : 6 + 2 * peers]
    (
        keep_out,
        send_out,
        col_out,
        row_idx,
        col_idx,
        diag,
        vec_rows,
        vec_cols,
        acc_rows,
        acc_cols,
        small_sems,
    ) = refs[6 + 2 * peers :]
    row = lax.axis_index("row")
    col = lax.axis_index("col")
    plane, core = col // 2, col % 2
    vectors = chip.shape[0] // 2
    width = tiles.shape[-1]
    piece_tiles = chip.shape[1] // width
    first = core == 0

    small = [
        pltpu.make_async_copy(source, target, small_sems.at[k])
        for k, (source, target) in enumerate(
            (
                (row_idx_hbm, row_idx),
                (col_idx_hbm, col_idx),
                (diag_hbm, diag),
            )
        )
    ]

    total = count[0, 0]
    groups = (total + group - 1) // group

    for copy in small:
        copy.start()
    acc_rows[...] = jnp.zeros_like(acc_rows)
    acc_cols[...] = jnp.zeros_like(acc_cols)

    def store_split(target, base, read):
        for t in range(piece_tiles):
            high, low = halves(read(slice(t * width, (t + 1) * width)))
            target[base + t] = jnp.concatenate([high, low], axis=0)

    for s in range(1, planes):
        base = jnp.bitwise_xor(plane, s) * 2 * piece_tiles
        for side in range(2):
            part = slice(side * vectors, (side + 1) * vectors)
            store_split(
                vec_rows,
                base + side * piece_tiles,
                lambda at: jnp.where(first, fetched[s - 1][part, at], passed[s - 1][part, at]),
            )
    for s in range(1, rows):
        store_split(
            vec_cols,
            jnp.bitwise_xor(row, s) * piece_tiles,
            lambda at: jnp.where(
                first, passed[s - 1][vectors:, at], fetched[s - 1][:vectors, at]
            ),
        )
    store_split(vec_rows, col * piece_tiles, lambda at: chip[:vectors, at])
    store_split(vec_rows, (col + 1 - 2 * core) * piece_tiles, lambda at: chip[vectors:, at])
    store_split(vec_cols, row * piece_tiles, lambda at: chip[:vectors, at])
    small[0].wait()
    small[1].wait()

    spare_row = acc_rows.shape[0] - 1
    spare_col = acc_cols.shape[0] - 1

    def multiply(g, carry):
        for k in range(group):
            m = g * group + k
            alive = m < total
            r, c = row_idx[0, 0, m], col_idx[0, 0, m]
            high, low = halves(tiles[m])
            from_row = vec_rows[r]
            from_col = vec_cols[c]
            back = jnp.dot(
                jnp.concatenate([from_row, from_row], axis=1),
                jnp.concatenate([high, low], axis=0),
                preferred_element_type=jnp.float32,
            )
            ahead = lax.dot_general(
                jnp.concatenate([high, low], axis=1),
                jnp.concatenate([from_col, from_col], axis=1),
                (((1,), (1,)), ((), ())),
                preferred_element_type=jnp.float32,
            ).T
            acc_rows[jnp.where(alive, r, spare_row)] += ahead[:8] + ahead[8:]
            acc_cols[jnp.where(alive, c, spare_col)] += back[:8] + back[8:]
        return carry

    lax.fori_loop(0, groups, multiply, 0)
    small[2].wait()

    for s in range(planes):
        base = jnp.bitwise_xor(plane, s) * 2 * piece_tiles
        for t in range(piece_tiles):
            at = slice(t * width, (t + 1) * width)
            keep_out[s, :, at] = acc_rows[base + core * piece_tiles + t]
            send_out[s, :, at] = acc_rows[base + (1 - core) * piece_tiles + t]
    for s in range(rows):
        base = jnp.bitwise_xor(row, s) * piece_tiles
        for t in range(piece_tiles):
            at = slice(t * width, (t + 1) * width)
            piece = acc_cols[base + t]
            if s == 0:
                piece = piece + chip[:vectors, at] * diag[:, at]
            col_out[s, :, at] = piece


def fixed_kernel(now, prev, out, both, sems):
    vectors = now.shape[0]
    copies = [
        pltpu.make_async_copy(now, both.at[pl.ds(0, vectors)], sems.at[0]),
        pltpu.make_async_copy(prev, both.at[pl.ds(vectors, vectors)], sems.at[1]),
    ]
    for copy in copies:
        copy.start()
    for copy in copies:
        copy.wait()
    out[...] = contract(both[...], both[...])


def add_kernel(block, arriving, out):
    half = out.shape[0]
    for s in range(half):
        out[s] = block[s] + arriving[s]


def sum_kernel(*refs):
    total = refs[0][...]
    for ref in refs[1:-1]:
        total = total + ref[...]
    refs[-1][...] = total


def image_kernel(copies, *refs):
    now, prev, fixed_in = refs[:3]
    image_out, sums_out = refs[-2:]
    image = refs[3][...]
    for ref in refs[4:-2]:
        image = image + ref[...]
    image_out[...] = image
    block, last = now[...], prev[...]
    vectors = image.shape[0]
    both = jnp.concatenate([block, last], axis=0)
    against = contract(image, jnp.concatenate([image, both], axis=0))
    fixed = fixed_in[...]
    half = sums_out.shape[2] // 2
    used = against.shape[1] + 2 * fixed.shape[1]
    sums = jnp.concatenate(
        [
            against,
            fixed[:vectors],
            fixed[vectors:],
            jnp.zeros((vectors, half - used), jnp.float32),
        ],
        axis=1,
    )
    sums = jnp.concatenate([sums[: vectors // 2], sums[vectors // 2 :]], axis=1)
    for k in range(copies):
        sums_out[k] = sums


def finish_kernel(states, sums_in, image, now, prev, coupling, next_out, alpha_out, beta_out):
    vectors = image.shape[0]
    sums = jnp.sum(sums_in[...], axis=0) / states
    half = sums.shape[1] // 2
    sums = jnp.concatenate([sums[:, :half], sums[:, half:]], axis=0)
    image_gram = sums[:, :vectors]
    alpha_t = sums[:, vectors : 2 * vectors]
    image_prev = sums[:, 2 * vectors : 3 * vectors]
    fixed = jnp.concatenate(
        [sums[:, 3 * vectors : 5 * vectors], sums[:, 5 * vectors : 7 * vectors]], axis=0
    )
    pair = coupling[...]
    left = jnp.concatenate([alpha_t, pair], axis=1)
    seen = jnp.concatenate([alpha_t, image_prev], axis=1)
    gram = image_gram + contract(
        jnp.concatenate([matmul(left, fixed) - seen, -left], axis=1),
        jnp.concatenate([left, seen], axis=1),
    )
    row_at = lax.broadcasted_iota(jnp.int32, (vectors, vectors), 0)
    col_at = lax.broadcasted_iota(jnp.int32, (vectors, vectors), 1)
    eye = (row_at == col_at).astype(jnp.float32)
    alpha_out[...] = contract(eye, alpha_t)
    work = jnp.concatenate([gram, eye, -left], axis=1)
    below = lax.broadcasted_iota(jnp.int32, (vectors, 1), 0)
    pivots = jnp.zeros((vectors, 1), jnp.float32)
    for j in range(vectors):
        pivot = work[j : j + 1, j : j + 1]
        line = work[j : j + 1, :]
        pivots = jnp.where(below == j, pivot, pivots)
        if j + 1 < vectors:
            factor = jnp.where(below > j, work[:, j : j + 1] / pivot, 0.0)
            work = work - factor * line
    work = work / jnp.sqrt(pivots)
    beta_out[...] = jnp.where(col_at >= row_at, work[:, :vectors], 0.0)
    next_out[...] = matmul(
        work[:, vectors:], jnp.concatenate([image[...], now[...], prev[...]], axis=0)
    )


def local(rows, cols, tiles, tile_rows, tile_cols, tile_counts, block_now, block_prev, coupling, diag_energy):
    slots, width = tiles.shape[2], tiles.shape[4]
    vectors, piece = block_now.shape
    piece_tiles = piece // width
    planes = cols // 2
    f32 = jnp.float32
    piece_shape = jax.ShapeDtypeStruct((vectors, piece), f32)

    def along_col(x, s):
        return lax.ppermute(x, "col", [(i, i ^ s) for i in range(cols)])

    def along_row(x, s):
        return lax.ppermute(x, "row", [(i, i ^ s) for i in range(rows)])

    def apart(x, s):
        pairs = []
        for r in range(rows):
            for c in range(cols):
                if c % 2 == 0:
                    to = (r, c ^ (2 * s) if s < planes else c)
                else:
                    to = (r ^ s if s < rows else r, c)
                pairs.append((r * cols + c, to[0] * cols + to[1]))
        return lax.ppermute(x, ("row", "col"), pairs)

    in_vmem = pl.BlockSpec(memory_space=VMEM)
    in_hbm = pl.BlockSpec(memory_space=pltpu.HBM)

    def stay(x):
        return pltpu.with_memory_space_constraint(x, pltpu.HBM)

    fixed = pl.pallas_call(
        fixed_kernel,
        out_shape=jax.ShapeDtypeStruct((2 * vectors, 2 * vectors), f32),
        in_specs=[in_hbm] * 2,
        out_specs=in_vmem,
        scratch_shapes=[
            VMEM((2 * vectors, piece), f32),
            pltpu.SemaphoreType.DMA((2,)),
        ],
        compiler_params=pltpu.CompilerParams(vmem_limit_bytes=16 * MIB),
        cost_estimate=pl.CostEstimate(
            flops=WAIT_FLOPS, bytes_accessed=2 * vectors * piece * 4, transcendentals=0
        ),
        name="fixed",
    )(stay(block_now), stay(block_prev))
    beside = along_col(block_now, 1)
    chip = jnp.concatenate([block_now, beside], axis=0)
    peers = range(1, max(planes, rows))
    fetched = [apart(chip, s) for s in peers]
    fetched[0], fixed = lax.optimization_barrier((fetched[0], fixed))
    passed = [along_col(x, 1) for x in fetched]

    group = math.gcd(slots, GROUP)

    keep, send, col_parts = pl.pallas_call(
        functools.partial(products_kernel, rows, planes, group),
        out_shape=(
            jax.ShapeDtypeStruct((planes, vectors, piece), f32),
            jax.ShapeDtypeStruct((planes, vectors, piece), f32),
            jax.ShapeDtypeStruct((rows, vectors, piece), f32),
        ),
        in_specs=[pl.BlockSpec(memory_space=SMEM)]
        + [in_vmem]
        + [in_hbm] * 3
        + [in_vmem] * (1 + 2 * len(peers)),
        out_specs=(in_vmem,) * 3,
        scratch_shapes=[
            SMEM(tile_rows.shape, jnp.int32),
            SMEM(tile_cols.shape, jnp.int32),
            VMEM((1, piece), f32),
            VMEM((cols * piece_tiles, 2 * vectors, width), jnp.bfloat16),
            VMEM((rows * piece_tiles, 2 * vectors, width), jnp.bfloat16),
            VMEM((cols * piece_tiles + 1, vectors, width), f32),
            VMEM((rows * piece_tiles + 1, vectors, width), f32),
            pltpu.SemaphoreType.DMA((3,)),
        ],
        compiler_params=pltpu.CompilerParams(vmem_limit_bytes=20 * MIB),
        name="products",
    )(
        tile_counts,
        pltpu.with_memory_space_constraint(tiles.reshape(slots, width, width), VMEM),
        stay(tile_rows),
        stay(tile_cols),
        stay(diag_energy.reshape(1, piece)),
        chip,
        *fetched,
        *passed,
    )

    block, half = col_parts, rows // 2
    arriving = along_row(block[half:], half)
    from_core = along_col(send, 1)
    summed = [keep[s] + from_core[s] for s in range(1, planes)]
    arriving, *_ = lax.optimization_barrier((arriving, *summed))
    back_planes = [along_col(x, 2 * s) for s, x in enumerate(summed, 1)]
    while half > 1:
        block = pl.pallas_call(
            add_kernel,
            out_shape=jax.ShapeDtypeStruct((half, vectors, piece), f32),
            in_specs=[in_vmem] * 2,
            out_specs=in_vmem,
            compiler_params=pltpu.CompilerParams(vmem_limit_bytes=16 * MIB),
            cost_estimate=pl.CostEstimate(
                flops=WAIT_FLOPS, bytes_accessed=3 * half * vectors * piece * 4, transcendentals=0
            ),
            name="add",
        )(block, arriving)
        half //= 2
        arriving = along_row(block[half:], half)
    most = pl.pallas_call(
        sum_kernel,
        out_shape=piece_shape,
        in_specs=[in_vmem] * (2 + planes),
        out_specs=in_vmem,
        compiler_params=pltpu.CompilerParams(vmem_limit_bytes=16 * MIB),
        cost_estimate=pl.CostEstimate(
            flops=WAIT_FLOPS, bytes_accessed=(3 + planes) * vectors * piece * 4, transcendentals=0
        ),
        name="sum",
    )(keep[0], from_core[0], block[0], *back_planes)
    terms = [most, arriving[0]]

    devices = rows * cols
    image, sums = pl.pallas_call(
        functools.partial(image_kernel, devices),
        out_shape=(
            piece_shape,
            jax.ShapeDtypeStruct((devices, vectors // 2, 128), f32),
        ),
        in_specs=[in_vmem] * (3 + len(terms)),
        out_specs=(in_vmem,) * 2,
        compiler_params=pltpu.CompilerParams(vmem_limit_bytes=16 * MIB),
        name="image",
    )(block_now, block_prev, fixed, *terms)

    sums = lax.all_to_all(sums, ("row", "col"), 0, 0)
    return pl.pallas_call(
        functools.partial(finish_kernel, float(piece * devices)),
        out_shape=(
            piece_shape,
            jax.ShapeDtypeStruct((vectors, vectors), f32),
            jax.ShapeDtypeStruct((vectors, vectors), f32),
        ),
        in_specs=[in_vmem] * 5,
        out_specs=(in_vmem,) * 3,
        compiler_params=pltpu.CompilerParams(vmem_limit_bytes=16 * MIB),
        name="finish",
    )(sums, image, block_now, block_prev, coupling)


def solution(mesh):
    return jax.shard_map(
        functools.partial(local, mesh.shape["row"], mesh.shape["col"]),
        mesh=mesh,
        in_specs=(
            P("row", "col", None, None, None),
            P("row", "col", None),
            P("row", "col", None),
            P("row", "col"),
            P(None, ("row", "col")),
            P(None, ("row", "col")),
            P(),
            P(("row", "col")),
        ),
        out_specs=(P(None, ("row", "col")), P(), P()),
        check_vma=False,
    )
```

```python
import functools
import math

import jax
import jax.numpy as jnp
from jax import lax
from jax.experimental import pallas as pl
from jax.experimental.pallas import tpu as pltpu
from jax.sharding import PartitionSpec as P

VMEM = pltpu.VMEM
SMEM = pltpu.SMEM
GROUP = 64
WAIT_FLOPS = 20_000_000_000
MIB = 1 << 20


def halves(x):
    high = x.astype(jnp.bfloat16)
    low = (x - high.astype(jnp.float32)).astype(jnp.bfloat16)
    return high, low


def contract(left, right):
    return lax.dot_general(
        left,
        right,
        (((1,), (1,)), ((), ())),
        precision=lax.Precision.HIGHEST,
        preferred_element_type=jnp.float32,
    )


def matmul(left, right):
    return jnp.dot(
        left, right, precision=lax.Precision.HIGHEST, preferred_element_type=jnp.float32
    )


def products_kernel(rows, planes, group, *refs):
    peers = max(planes, rows) - 1
    count, tiles, row_idx_hbm, col_idx_hbm, diag_hbm, chip = refs[:6]
    fetched = refs[6 : 6 + peers]
    passed = refs[6 + peers : 6 + 2 * peers]
    (
        keep_out,
        send_out,
        col_out,
        row_idx,
        col_idx,
        diag,
        vec_rows,
        vec_cols,
        acc_rows,
        acc_cols,
        small_sems,
    ) = refs[6 + 2 * peers :]
    row = lax.axis_index("row")
    col = lax.axis_index("col")
    plane, core = col // 2, col % 2
    vectors = chip.shape[0] // 2
    width = tiles.shape[-1]
    piece_tiles = chip.shape[1] // width
    first = core == 0

    small = [
        pltpu.make_async_copy(source, target, small_sems.at[k])
        for k, (source, target) in enumerate(
            (
                (row_idx_hbm, row_idx),
                (col_idx_hbm, col_idx),
                (diag_hbm, diag),
            )
        )
    ]

    total = count[0, 0]
    groups = (total + group - 1) // group

    for copy in small:
        copy.start()
    acc_rows[...] = jnp.zeros_like(acc_rows)
    acc_cols[...] = jnp.zeros_like(acc_cols)

    def store_split(target, base, read):
        for t in range(piece_tiles):
            high, low = halves(read(slice(t * width, (t + 1) * width)))
            target[base + t] = jnp.concatenate([high, low], axis=0)

    for s in range(1, planes):
        base = jnp.bitwise_xor(plane, s) * 2 * piece_tiles
        for side in range(2):
            part = slice(side * vectors, (side + 1) * vectors)
            store_split(
                vec_rows,
                base + side * piece_tiles,
                lambda at: jnp.where(first, fetched[s - 1][part, at], passed[s - 1][part, at]),
            )
    for s in range(1, rows):
        store_split(
            vec_cols,
            jnp.bitwise_xor(row, s) * piece_tiles,
            lambda at: jnp.where(
                first, passed[s - 1][vectors:, at], fetched[s - 1][:vectors, at]
            ),
        )
    store_split(vec_rows, col * piece_tiles, lambda at: chip[:vectors, at])
    store_split(vec_rows, (col + 1 - 2 * core) * piece_tiles, lambda at: chip[vectors:, at])
    store_split(vec_cols, row * piece_tiles, lambda at: chip[:vectors, at])
    small[0].wait()
    small[1].wait()

    spare_row = acc_rows.shape[0] - 1
    spare_col = acc_cols.shape[0] - 1

    def multiply(g, carry):
        for k in range(group):
            m = g * group + k
            alive = m < total
            r, c = row_idx[0, 0, m], col_idx[0, 0, m]
            high, low = halves(tiles[m])
            from_row = vec_rows[r]
            from_col = vec_cols[c]
            back = jnp.dot(
                jnp.concatenate([from_row, from_row], axis=1),
                jnp.concatenate([high, low], axis=0),
                preferred_element_type=jnp.float32,
            )
            ahead = lax.dot_general(
                jnp.concatenate([high, low], axis=1),
                jnp.concatenate([from_col, from_col], axis=1),
                (((1,), (1,)), ((), ())),
                preferred_element_type=jnp.float32,
            ).T
            acc_rows[jnp.where(alive, r, spare_row)] += ahead[:8] + ahead[8:]
            acc_cols[jnp.where(alive, c, spare_col)] += back[:8] + back[8:]
        return carry

    lax.fori_loop(0, groups, multiply, 0)
    small[2].wait()

    for s in range(planes):
        base = jnp.bitwise_xor(plane, s) * 2 * piece_tiles
        for t in range(piece_tiles):
            at = slice(t * width, (t + 1) * width)
            keep_out[s, :, at] = acc_rows[base + core * piece_tiles + t]
            send_out[s, :, at] = acc_rows[base + (1 - core) * piece_tiles + t]
    for s in range(rows):
        base = jnp.bitwise_xor(row, s) * piece_tiles
        for t in range(piece_tiles):
            at = slice(t * width, (t + 1) * width)
            piece = acc_cols[base + t]
            if s == 0:
                piece = piece + chip[:vectors, at] * diag[:, at]
            col_out[s, :, at] = piece


def fixed_kernel(count, now, prev, out, both, sems):
    vectors = now.shape[0]
    copies = [
        pltpu.make_async_copy(now, both.at[pl.ds(0, vectors)], sems.at[0]),
        pltpu.make_async_copy(prev, both.at[pl.ds(vectors, vectors)], sems.at[1]),
    ]
    for copy in copies:
        copy.start()
    for copy in copies:
        copy.wait()
    out[...] = contract(both[...], both[...])


def image_kernel(copies, *refs):
    now, prev, fixed_in = refs[:3]
    image_out, sums_out = refs[-2:]
    image = refs[3][...]
    for ref in refs[4:-2]:
        image = image + ref[...]
    image_out[...] = image
    block, last = now[...], prev[...]
    vectors = image.shape[0]
    both = jnp.concatenate([block, last], axis=0)
    against = contract(image, jnp.concatenate([image, both], axis=0))
    fixed = fixed_in[...]
    half = sums_out.shape[2] // 2
    used = against.shape[1] + 2 * fixed.shape[1]
    sums = jnp.concatenate(
        [
            against,
            fixed[:vectors],
            fixed[vectors:],
            jnp.zeros((vectors, half - used), jnp.float32),
        ],
        axis=1,
    )
    sums = jnp.concatenate([sums[: vectors // 2], sums[vectors // 2 :]], axis=1)
    for k in range(copies):
        sums_out[k] = sums


def finish_kernel(states, sums_in, image, now, prev, coupling, next_out, alpha_out, beta_out):
    vectors = image.shape[0]
    sums = jnp.sum(sums_in[...], axis=0) / states
    half = sums.shape[1] // 2
    sums = jnp.concatenate([sums[:, :half], sums[:, half:]], axis=0)
    image_gram = sums[:, :vectors]
    alpha_t = sums[:, vectors : 2 * vectors]
    image_prev = sums[:, 2 * vectors : 3 * vectors]
    fixed = jnp.concatenate(
        [sums[:, 3 * vectors : 5 * vectors], sums[:, 5 * vectors : 7 * vectors]], axis=0
    )
    pair = coupling[...]
    left = jnp.concatenate([alpha_t, pair], axis=1)
    seen = jnp.concatenate([alpha_t, image_prev], axis=1)
    gram = image_gram + contract(
        jnp.concatenate([matmul(left, fixed) - seen, -left], axis=1),
        jnp.concatenate([left, seen], axis=1),
    )
    row_at = lax.broadcasted_iota(jnp.int32, (vectors, vectors), 0)
    col_at = lax.broadcasted_iota(jnp.int32, (vectors, vectors), 1)
    eye = (row_at == col_at).astype(jnp.float32)
    alpha_out[...] = contract(eye, alpha_t)
    work = jnp.concatenate([gram, eye, -left], axis=1)
    below = lax.broadcasted_iota(jnp.int32, (vectors, 1), 0)
    pivots = jnp.zeros((vectors, 1), jnp.float32)
    for j in range(vectors):
        pivot = work[j : j + 1, j : j + 1]
        line = work[j : j + 1, :]
        pivots = jnp.where(below == j, pivot, pivots)
        if j + 1 < vectors:
            factor = jnp.where(below > j, work[:, j : j + 1] / pivot, 0.0)
            work = work - factor * line
    work = work / jnp.sqrt(pivots)
    beta_out[...] = jnp.where(col_at >= row_at, work[:, :vectors], 0.0)
    next_out[...] = matmul(
        work[:, vectors:], jnp.concatenate([image[...], now[...], prev[...]], axis=0)
    )


def local(rows, cols, tiles, tile_rows, tile_cols, tile_counts, block_now, block_prev, coupling, diag_energy):
    slots, width = tiles.shape[2], tiles.shape[4]
    vectors, piece = block_now.shape
    piece_tiles = piece // width
    planes = cols // 2
    f32 = jnp.float32
    piece_shape = jax.ShapeDtypeStruct((vectors, piece), f32)

    def along_col(x, s):
        return lax.ppermute(x, "col", [(i, i ^ s) for i in range(cols)])

    def along_row(x, s):
        return lax.ppermute(x, "row", [(i, i ^ s) for i in range(rows)])

    def apart(x, s):
        pairs = []
        for r in range(rows):
            for c in range(cols):
                if c % 2 == 0:
                    to = (r, c ^ (2 * s) if s < planes else c)
                else:
                    to = (r ^ s if s < rows else r, c)
                pairs.append((r * cols + c, to[0] * cols + to[1]))
        return lax.ppermute(x, ("row", "col"), pairs)

    in_vmem = pl.BlockSpec(memory_space=VMEM)
    in_hbm = pl.BlockSpec(memory_space=pltpu.HBM)

    def stay(x):
        return pltpu.with_memory_space_constraint(x, pltpu.HBM)

    fixed = pl.pallas_call(
        fixed_kernel,
        out_shape=jax.ShapeDtypeStruct((2 * vectors, 2 * vectors), f32),
        in_specs=[pl.BlockSpec(memory_space=SMEM)] + [in_hbm] * 2,
        out_specs=in_vmem,
        scratch_shapes=[
            VMEM((2 * vectors, piece), f32),
            pltpu.SemaphoreType.DMA((2,)),
        ],
        compiler_params=pltpu.CompilerParams(vmem_limit_bytes=16 * MIB),
        cost_estimate=pl.CostEstimate(
            flops=WAIT_FLOPS, bytes_accessed=2 * vectors * piece * 4, transcendentals=0
        ),
        name="fixed",
    )(tile_counts, stay(block_now), stay(block_prev))
    beside = along_col(block_now, 1)
    chip = jnp.concatenate([block_now, beside], axis=0)
    peers = range(1, max(planes, rows))
    fetched = [apart(chip, s) for s in peers]
    fetched[0], fixed = lax.optimization_barrier((fetched[0], fixed))
    passed = [along_col(x, 1) for x in fetched]

    group = math.gcd(slots, GROUP)

    keep, send, col_parts = pl.pallas_call(
        functools.partial(products_kernel, rows, planes, group),
        out_shape=(
            jax.ShapeDtypeStruct((planes, vectors, piece), f32),
            jax.ShapeDtypeStruct((planes, vectors, piece), f32),
            jax.ShapeDtypeStruct((rows, vectors, piece), f32),
        ),
        in_specs=[pl.BlockSpec(memory_space=SMEM)]
        + [in_vmem]
        + [in_hbm] * 3
        + [in_vmem] * (1 + 2 * len(peers)),
        out_specs=(in_vmem,) * 3,
        scratch_shapes=[
            SMEM(tile_rows.shape, jnp.int32),
            SMEM(tile_cols.shape, jnp.int32),
            VMEM((1, piece), f32),
            VMEM((cols * piece_tiles, 2 * vectors, width), jnp.bfloat16),
            VMEM((rows * piece_tiles, 2 * vectors, width), jnp.bfloat16),
            VMEM((cols * piece_tiles + 1, vectors, width), f32),
            VMEM((rows * piece_tiles + 1, vectors, width), f32),
            pltpu.SemaphoreType.DMA((3,)),
        ],
        compiler_params=pltpu.CompilerParams(vmem_limit_bytes=20 * MIB),
        name="products",
    )(
        tile_counts,
        pltpu.with_memory_space_constraint(tiles.reshape(slots, width, width), VMEM),
        stay(tile_rows),
        stay(tile_cols),
        stay(diag_energy.reshape(1, piece)),
        chip,
        *fetched,
        *passed,
    )

    from_core = along_col(send, 1)
    summed = [keep[s] + from_core[s] for s in range(1, planes)]
    nearest, *summed = lax.optimization_barrier((col_parts[1], *summed))
    back_rows = [along_row(nearest, 1)]
    back_rows += [along_row(col_parts[s], s) for s in range(2, rows)]
    back_planes = [along_col(summed[s - 1], 2 * s) for s in range(1, planes)]
    terms = [keep[0], from_core[0], col_parts[0], *back_planes[:-1]]
    terms += [back_rows[0], back_planes[-1], *back_rows[1:]]

    devices = rows * cols
    image, sums = pl.pallas_call(
        functools.partial(image_kernel, devices),
        out_shape=(
            piece_shape,
            jax.ShapeDtypeStruct((devices, vectors // 2, 128), f32),
        ),
        in_specs=[in_vmem] * (3 + len(terms)),
        out_specs=(in_vmem,) * 2,
        compiler_params=pltpu.CompilerParams(vmem_limit_bytes=16 * MIB),
        name="image",
    )(block_now, block_prev, fixed, *terms)

    sums = lax.all_to_all(sums, ("row", "col"), 0, 0)
    return pl.pallas_call(
        functools.partial(finish_kernel, float(piece * devices)),
        out_shape=(
            piece_shape,
            jax.ShapeDtypeStruct((vectors, vectors), f32),
            jax.ShapeDtypeStruct((vectors, vectors), f32),
        ),
        in_specs=[in_vmem] * 5,
        out_specs=(in_vmem,) * 3,
        compiler_params=pltpu.CompilerParams(vmem_limit_bytes=16 * MIB),
        name="finish",
    )(sums, image, block_now, block_prev, coupling)


def solution(mesh):
    return jax.shard_map(
        functools.partial(local, mesh.shape["row"], mesh.shape["col"]),
        mesh=mesh,
        in_specs=(
            P("row", "col", None, None, None),
            P("row", "col", None),
            P("row", "col", None),
            P("row", "col"),
            P(None, ("row", "col")),
            P(None, ("row", "col")),
            P(),
            P(("row", "col")),
        ),
        out_specs=(P(None, ("row", "col")), P(), P()),
        check_vma=False,
    )
```

```python
import functools
import math

import jax
import jax.numpy as jnp
from jax import lax
from jax.experimental import pallas as pl
from jax.experimental.pallas import tpu as pltpu
from jax.sharding import PartitionSpec as P

VMEM = pltpu.VMEM
SMEM = pltpu.SMEM
GROUP = 64
WAIT_FLOPS = 20_000_000_000
MIB = 1 << 20


def halves(x):
    high = x.astype(jnp.bfloat16)
    low = (x - high.astype(jnp.float32)).astype(jnp.bfloat16)
    return high, low


def contract(left, right):
    return lax.dot_general(
        left,
        right,
        (((1,), (1,)), ((), ())),
        precision=lax.Precision.HIGHEST,
        preferred_element_type=jnp.float32,
    )


def matmul(left, right):
    return jnp.dot(
        left, right, precision=lax.Precision.HIGHEST, preferred_element_type=jnp.float32
    )


def products_kernel(rows, planes, group, *refs):
    peers = max(planes, rows) - 1
    count, tiles, row_idx_hbm, col_idx_hbm, diag_hbm, chip = refs[:6]
    fetched = refs[6 : 6 + peers]
    passed = refs[6 + peers : 6 + 2 * peers]
    (
        keep_out,
        send_out,
        col_out,
        row_idx,
        col_idx,
        diag,
        vec_rows,
        vec_cols,
        acc_rows,
        acc_cols,
        small_sems,
    ) = refs[6 + 2 * peers :]
    row = lax.axis_index("row")
    col = lax.axis_index("col")
    plane, core = col // 2, col % 2
    vectors = chip.shape[0] // 2
    width = tiles.shape[-1]
    piece_tiles = chip.shape[1] // width
    first = core == 0

    small = [
        pltpu.make_async_copy(source, target, small_sems.at[k])
        for k, (source, target) in enumerate(
            (
                (row_idx_hbm, row_idx),
                (col_idx_hbm, col_idx),
                (diag_hbm, diag),
            )
        )
    ]

    total = count[0, 0]
    groups = (total + group - 1) // group

    for copy in small:
        copy.start()
    acc_rows[...] = jnp.zeros_like(acc_rows)
    acc_cols[...] = jnp.zeros_like(acc_cols)

    def store_split(target, base, read):
        for t in range(piece_tiles):
            high, low = halves(read(slice(t * width, (t + 1) * width)))
            target[base + t] = jnp.concatenate([high, low], axis=0)

    for s in range(1, planes):
        base = jnp.bitwise_xor(plane, s) * 2 * piece_tiles
        for side in range(2):
            part = slice(side * vectors, (side + 1) * vectors)
            store_split(
                vec_rows,
                base + side * piece_tiles,
                lambda at: jnp.where(first, fetched[s - 1][part, at], passed[s - 1][part, at]),
            )
    for s in range(1, rows):
        store_split(
            vec_cols,
            jnp.bitwise_xor(row, s) * piece_tiles,
            lambda at: jnp.where(
                first, passed[s - 1][vectors:, at], fetched[s - 1][:vectors, at]
            ),
        )
    store_split(vec_rows, col * piece_tiles, lambda at: chip[:vectors, at])
    store_split(vec_rows, (col + 1 - 2 * core) * piece_tiles, lambda at: chip[vectors:, at])
    store_split(vec_cols, row * piece_tiles, lambda at: chip[:vectors, at])
    small[0].wait()
    small[1].wait()

    spare_row = acc_rows.shape[0] - 1
    spare_col = acc_cols.shape[0] - 1

    def multiply(g, carry):
        for k in range(group):
            m = g * group + k
            alive = m < total
            r, c = row_idx[0, 0, m], col_idx[0, 0, m]
            high, low = halves(tiles[m])
            from_row = vec_rows[r]
            from_col = vec_cols[c]
            back = jnp.dot(
                jnp.concatenate([from_row, from_row], axis=1),
                jnp.concatenate([high, low], axis=0),
                preferred_element_type=jnp.float32,
            )
            ahead = lax.dot_general(
                jnp.concatenate([high, low], axis=1),
                jnp.concatenate([from_col, from_col], axis=1),
                (((1,), (1,)), ((), ())),
                preferred_element_type=jnp.float32,
            ).T
            acc_rows[jnp.where(alive, r, spare_row)] += ahead[:8] + ahead[8:]
            acc_cols[jnp.where(alive, c, spare_col)] += back[:8] + back[8:]
        return carry

    lax.fori_loop(0, groups, multiply, 0)
    small[2].wait()

    for s in range(planes):
        base = jnp.bitwise_xor(plane, s) * 2 * piece_tiles
        for t in range(piece_tiles):
            at = slice(t * width, (t + 1) * width)
            keep_out[s, :, at] = acc_rows[base + core * piece_tiles + t]
            send_out[s, :, at] = acc_rows[base + (1 - core) * piece_tiles + t]
    for s in range(rows):
        base = lax.rem(row + rows - s, rows) * piece_tiles
        for t in range(piece_tiles):
            at = slice(t * width, (t + 1) * width)
            piece = acc_cols[base + t]
            if s == 0:
                piece = piece + chip[:vectors, at] * diag[:, at]
            col_out[s, :, at] = piece


def fixed_kernel(now, prev, out, both, sems):
    vectors = now.shape[0]
    copies = [
        pltpu.make_async_copy(now, both.at[pl.ds(0, vectors)], sems.at[0]),
        pltpu.make_async_copy(prev, both.at[pl.ds(vectors, vectors)], sems.at[1]),
    ]
    for copy in copies:
        copy.start()
    for copy in copies:
        copy.wait()
    out[...] = contract(both[...], both[...])


def image_kernel(copies, *refs):
    now, prev, fixed_in = refs[:3]
    image_out, sums_out = refs[-2:]
    image = refs[3][...]
    for ref in refs[4:-2]:
        image = image + ref[...]
    image_out[...] = image
    block, last = now[...], prev[...]
    vectors = image.shape[0]
    both = jnp.concatenate([block, last], axis=0)
    against = contract(image, jnp.concatenate([image, both], axis=0))
    fixed = fixed_in[...]
    half = sums_out.shape[2] // 2
    used = against.shape[1] + 2 * fixed.shape[1]
    sums = jnp.concatenate(
        [
            against,
            fixed[:vectors],
            fixed[vectors:],
            jnp.zeros((vectors, half - used), jnp.float32),
        ],
        axis=1,
    )
    sums = jnp.concatenate([sums[: vectors // 2], sums[vectors // 2 :]], axis=1)
    for k in range(copies):
        sums_out[k] = sums


def finish_kernel(states, sums_in, image, now, prev, coupling, next_out, alpha_out, beta_out):
    vectors = image.shape[0]
    sums = jnp.sum(sums_in[...], axis=0) / states
    half = sums.shape[1] // 2
    sums = jnp.concatenate([sums[:, :half], sums[:, half:]], axis=0)
    image_gram = sums[:, :vectors]
    alpha_t = sums[:, vectors : 2 * vectors]
    image_prev = sums[:, 2 * vectors : 3 * vectors]
    fixed = jnp.concatenate(
        [sums[:, 3 * vectors : 5 * vectors], sums[:, 5 * vectors : 7 * vectors]], axis=0
    )
    pair = coupling[...]
    left = jnp.concatenate([alpha_t, pair], axis=1)
    seen = jnp.concatenate([alpha_t, image_prev], axis=1)
    gram = image_gram + contract(
        jnp.concatenate([matmul(left, fixed) - seen, -left], axis=1),
        jnp.concatenate([left, seen], axis=1),
    )
    row_at = lax.broadcasted_iota(jnp.int32, (vectors, vectors), 0)
    col_at = lax.broadcasted_iota(jnp.int32, (vectors, vectors), 1)
    eye = (row_at == col_at).astype(jnp.float32)
    alpha_out[...] = contract(eye, alpha_t)
    work = jnp.concatenate([gram, eye, -left], axis=1)
    below = lax.broadcasted_iota(jnp.int32, (vectors, 1), 0)
    pivots = jnp.zeros((vectors, 1), jnp.float32)
    for j in range(vectors):
        pivot = work[j : j + 1, j : j + 1]
        line = work[j : j + 1, :]
        pivots = jnp.where(below == j, pivot, pivots)
        if j + 1 < vectors:
            factor = jnp.where(below > j, work[:, j : j + 1] / pivot, 0.0)
            work = work - factor * line
    work = work / jnp.sqrt(pivots)
    beta_out[...] = jnp.where(col_at >= row_at, work[:, :vectors], 0.0)
    next_out[...] = matmul(
        work[:, vectors:], jnp.concatenate([image[...], now[...], prev[...]], axis=0)
    )


def local(rows, cols, tiles, tile_rows, tile_cols, tile_counts, block_now, block_prev, coupling, diag_energy):
    slots, width = tiles.shape[2], tiles.shape[4]
    vectors, piece = block_now.shape
    piece_tiles = piece // width
    planes = cols // 2
    f32 = jnp.float32
    piece_shape = jax.ShapeDtypeStruct((vectors, piece), f32)

    def along_col(x, s):
        return lax.ppermute(x, "col", [(i, i ^ s) for i in range(cols)])

    def along_row(x, s):
        return lax.ppermute(x, "row", [(i, (i - s) % rows) for i in range(rows)])

    def apart(x, s):
        pairs = []
        for r in range(rows):
            for c in range(cols):
                if c % 2 == 0:
                    to = (r, c ^ (2 * s) if s < planes else c)
                else:
                    to = (r ^ s if s < rows else r, c)
                pairs.append((r * cols + c, to[0] * cols + to[1]))
        return lax.ppermute(x, ("row", "col"), pairs)

    in_vmem = pl.BlockSpec(memory_space=VMEM)
    in_hbm = pl.BlockSpec(memory_space=pltpu.HBM)

    def stay(x):
        return pltpu.with_memory_space_constraint(x, pltpu.HBM)

    fixed = pl.pallas_call(
        fixed_kernel,
        out_shape=jax.ShapeDtypeStruct((2 * vectors, 2 * vectors), f32),
        in_specs=[in_hbm] * 2,
        out_specs=in_vmem,
        scratch_shapes=[
            VMEM((2 * vectors, piece), f32),
            pltpu.SemaphoreType.DMA((2,)),
        ],
        compiler_params=pltpu.CompilerParams(vmem_limit_bytes=16 * MIB),
        cost_estimate=pl.CostEstimate(
            flops=WAIT_FLOPS, bytes_accessed=2 * vectors * piece * 4, transcendentals=0
        ),
        name="fixed",
    )(stay(block_now), stay(block_prev))
    beside = along_col(block_now, 1)
    chip = jnp.concatenate([block_now, beside], axis=0)
    peers = range(1, max(planes, rows))
    fetched = [apart(chip, s) for s in peers]
    fetched[0], fixed = lax.optimization_barrier((fetched[0], fixed))
    passed = [along_col(x, 1) for x in fetched]

    group = math.gcd(slots, GROUP)

    keep, send, col_parts = pl.pallas_call(
        functools.partial(products_kernel, rows, planes, group),
        out_shape=(
            jax.ShapeDtypeStruct((planes, vectors, piece), f32),
            jax.ShapeDtypeStruct((planes, vectors, piece), f32),
            jax.ShapeDtypeStruct((rows, vectors, piece), f32),
        ),
        in_specs=[pl.BlockSpec(memory_space=SMEM)]
        + [in_vmem]
        + [in_hbm] * 3
        + [in_vmem] * (1 + 2 * len(peers)),
        out_specs=(in_vmem,) * 3,
        scratch_shapes=[
            SMEM(tile_rows.shape, jnp.int32),
            SMEM(tile_cols.shape, jnp.int32),
            VMEM((1, piece), f32),
            VMEM((cols * piece_tiles, 2 * vectors, width), jnp.bfloat16),
            VMEM((rows * piece_tiles, 2 * vectors, width), jnp.bfloat16),
            VMEM((cols * piece_tiles + 1, vectors, width), f32),
            VMEM((rows * piece_tiles + 1, vectors, width), f32),
            pltpu.SemaphoreType.DMA((3,)),
        ],
        compiler_params=pltpu.CompilerParams(vmem_limit_bytes=20 * MIB),
        name="products",
    )(
        tile_counts,
        pltpu.with_memory_space_constraint(tiles.reshape(slots, width, width), VMEM),
        stay(tile_rows),
        stay(tile_cols),
        stay(diag_energy.reshape(1, piece)),
        chip,
        *fetched,
        *passed,
    )

    back_rows = [along_row(col_parts[s], s) for s in range(1, rows)]
    from_core = along_col(send, 1)
    summed = [keep[s] + from_core[s] for s in range(1, planes)]
    back_planes = [along_col(summed[s - 1], 2 * s) for s in range(1, planes)]
    terms = [keep[0], from_core[0], col_parts[0], *back_planes, *back_rows]

    devices = rows * cols
    image, sums = pl.pallas_call(
        functools.partial(image_kernel, devices),
        out_shape=(
            piece_shape,
            jax.ShapeDtypeStruct((devices, vectors // 2, 128), f32),
        ),
        in_specs=[in_vmem] * (3 + len(terms)),
        out_specs=(in_vmem,) * 2,
        compiler_params=pltpu.CompilerParams(vmem_limit_bytes=16 * MIB),
        name="image",
    )(block_now, block_prev, fixed, *terms)

    sums = lax.all_to_all(sums, ("row", "col"), 0, 0)
    return pl.pallas_call(
        functools.partial(finish_kernel, float(piece * devices)),
        out_shape=(
            piece_shape,
            jax.ShapeDtypeStruct((vectors, vectors), f32),
            jax.ShapeDtypeStruct((vectors, vectors), f32),
        ),
        in_specs=[in_vmem] * 5,
        out_specs=(in_vmem,) * 3,
        compiler_params=pltpu.CompilerParams(vmem_limit_bytes=16 * MIB),
        name="finish",
    )(sums, image, block_now, block_prev, coupling)


def solution(mesh):
    return jax.shard_map(
        functools.partial(local, mesh.shape["row"], mesh.shape["col"]),
        mesh=mesh,
        in_specs=(
            P("row", "col", None, None, None),
            P("row", "col", None),
            P("row", "col", None),
            P("row", "col"),
            P(None, ("row", "col")),
            P(None, ("row", "col")),
            P(),
            P(("row", "col")),
        ),
        out_specs=(P(None, ("row", "col")), P(), P()),
        check_vma=False,
    )
```

```python
import functools
import math

import jax
import jax.numpy as jnp
from jax import lax
from jax.experimental import pallas as pl
from jax.experimental.pallas import tpu as pltpu
from jax.sharding import PartitionSpec as P

VMEM = pltpu.VMEM
SMEM = pltpu.SMEM
GROUP = 64
WAIT_FLOPS = 20_000_000_000
MIB = 1 << 20


def halves(x):
    high = x.astype(jnp.bfloat16)
    low = (x - high.astype(jnp.float32)).astype(jnp.bfloat16)
    return high, low


def contract(left, right):
    return lax.dot_general(
        left,
        right,
        (((1,), (1,)), ((), ())),
        precision=lax.Precision.HIGHEST,
        preferred_element_type=jnp.float32,
    )


def matmul(left, right):
    return jnp.dot(
        left, right, precision=lax.Precision.HIGHEST, preferred_element_type=jnp.float32
    )


def products_kernel(rows, planes, group, *refs):
    peers = max(planes, rows) - 1
    count, tiles, row_idx_hbm, col_idx_hbm, diag_hbm, chip = refs[:6]
    fetched = refs[6 : 6 + peers]
    passed = refs[6 + peers : 6 + 2 * peers]
    (
        keep_out,
        send_out,
        col_out,
        row_idx,
        col_idx,
        diag,
        vec_rows,
        vec_cols,
        acc_rows,
        acc_cols,
        small_sems,
    ) = refs[6 + 2 * peers :]
    row = lax.axis_index("row")
    col = lax.axis_index("col")
    plane, core = col // 2, col % 2
    vectors = chip.shape[0] // 2
    width = tiles.shape[-1]
    piece_tiles = chip.shape[1] // width
    first = core == 0

    small = [
        pltpu.make_async_copy(source, target, small_sems.at[k])
        for k, (source, target) in enumerate(
            (
                (row_idx_hbm, row_idx),
                (col_idx_hbm, col_idx),
                (diag_hbm, diag),
            )
        )
    ]

    total = count[0, 0]
    groups = (total + group - 1) // group

    for copy in small:
        copy.start()
    acc_rows[...] = jnp.zeros_like(acc_rows)
    acc_cols[...] = jnp.zeros_like(acc_cols)

    def store_split(target, base, read):
        for t in range(piece_tiles):
            high, low = halves(read(slice(t * width, (t + 1) * width)))
            target[base + t] = jnp.concatenate([high, low], axis=0)

    for s in range(1, planes):
        base = jnp.bitwise_xor(plane, s) * 2 * piece_tiles
        for side in range(2):
            part = slice(side * vectors, (side + 1) * vectors)
            store_split(
                vec_rows,
                base + side * piece_tiles,
                lambda at: jnp.where(first, fetched[s - 1][part, at], passed[s - 1][part, at]),
            )
    for s in range(1, rows):
        store_split(
            vec_cols,
            lax.rem(row + s, rows) * piece_tiles,
            lambda at: jnp.where(
                first, passed[s - 1][vectors:, at], fetched[s - 1][:vectors, at]
            ),
        )
    store_split(vec_rows, col * piece_tiles, lambda at: chip[:vectors, at])
    store_split(vec_rows, (col + 1 - 2 * core) * piece_tiles, lambda at: chip[vectors:, at])
    store_split(vec_cols, row * piece_tiles, lambda at: chip[:vectors, at])
    small[0].wait()
    small[1].wait()

    spare_row = acc_rows.shape[0] - 1
    spare_col = acc_cols.shape[0] - 1

    def multiply(g, carry):
        for k in range(group):
            m = g * group + k
            alive = m < total
            r, c = row_idx[0, 0, m], col_idx[0, 0, m]
            high, low = halves(tiles[m])
            from_row = vec_rows[r]
            from_col = vec_cols[c]
            back = jnp.dot(
                jnp.concatenate([from_row, from_row], axis=1),
                jnp.concatenate([high, low], axis=0),
                preferred_element_type=jnp.float32,
            )
            ahead = lax.dot_general(
                jnp.concatenate([high, low], axis=1),
                jnp.concatenate([from_col, from_col], axis=1),
                (((1,), (1,)), ((), ())),
                preferred_element_type=jnp.float32,
            ).T
            acc_rows[jnp.where(alive, r, spare_row)] += ahead[:8] + ahead[8:]
            acc_cols[jnp.where(alive, c, spare_col)] += back[:8] + back[8:]
        return carry

    lax.fori_loop(0, groups, multiply, 0)
    small[2].wait()

    for s in range(planes):
        base = jnp.bitwise_xor(plane, s) * 2 * piece_tiles
        for t in range(piece_tiles):
            at = slice(t * width, (t + 1) * width)
            keep_out[s, :, at] = acc_rows[base + core * piece_tiles + t]
            send_out[s, :, at] = acc_rows[base + (1 - core) * piece_tiles + t]
    for s in range(rows):
        base = lax.rem(row + rows - s, rows) * piece_tiles
        for t in range(piece_tiles):
            at = slice(t * width, (t + 1) * width)
            piece = acc_cols[base + t]
            if s == 0:
                piece = piece + chip[:vectors, at] * diag[:, at]
            col_out[s, :, at] = piece


def fixed_kernel(now, prev, out, both, sems):
    vectors = now.shape[0]
    copies = [
        pltpu.make_async_copy(now, both.at[pl.ds(0, vectors)], sems.at[0]),
        pltpu.make_async_copy(prev, both.at[pl.ds(vectors, vectors)], sems.at[1]),
    ]
    for copy in copies:
        copy.start()
    for copy in copies:
        copy.wait()
    out[...] = contract(both[...], both[...])


def image_kernel(copies, *refs):
    now, prev, fixed_in = refs[:3]
    image_out, sums_out = refs[-2:]
    image = refs[3][...]
    for ref in refs[4:-2]:
        image = image + ref[...]
    image_out[...] = image
    block, last = now[...], prev[...]
    vectors = image.shape[0]
    both = jnp.concatenate([block, last], axis=0)
    against = contract(image, jnp.concatenate([image, both], axis=0))
    fixed = fixed_in[...]
    half = sums_out.shape[2] // 2
    used = against.shape[1] + 2 * fixed.shape[1]
    sums = jnp.concatenate(
        [
            against,
            fixed[:vectors],
            fixed[vectors:],
            jnp.zeros((vectors, half - used), jnp.float32),
        ],
        axis=1,
    )
    sums = jnp.concatenate([sums[: vectors // 2], sums[vectors // 2 :]], axis=1)
    for k in range(copies):
        sums_out[k] = sums


def finish_kernel(states, sums_in, image, now, prev, coupling, next_out, alpha_out, beta_out):
    vectors = image.shape[0]
    sums = jnp.sum(sums_in[...], axis=0) / states
    half = sums.shape[1] // 2
    sums = jnp.concatenate([sums[:, :half], sums[:, half:]], axis=0)
    image_gram = sums[:, :vectors]
    alpha_t = sums[:, vectors : 2 * vectors]
    image_prev = sums[:, 2 * vectors : 3 * vectors]
    fixed = jnp.concatenate(
        [sums[:, 3 * vectors : 5 * vectors], sums[:, 5 * vectors : 7 * vectors]], axis=0
    )
    pair = coupling[...]
    left = jnp.concatenate([alpha_t, pair], axis=1)
    seen = jnp.concatenate([alpha_t, image_prev], axis=1)
    gram = image_gram + contract(
        jnp.concatenate([matmul(left, fixed) - seen, -left], axis=1),
        jnp.concatenate([left, seen], axis=1),
    )
    row_at = lax.broadcasted_iota(jnp.int32, (vectors, vectors), 0)
    col_at = lax.broadcasted_iota(jnp.int32, (vectors, vectors), 1)
    eye = (row_at == col_at).astype(jnp.float32)
    alpha_out[...] = contract(eye, alpha_t)
    work = jnp.concatenate([gram, eye, -left], axis=1)
    below = lax.broadcasted_iota(jnp.int32, (vectors, 1), 0)
    pivots = jnp.zeros((vectors, 1), jnp.float32)
    for j in range(vectors):
        pivot = work[j : j + 1, j : j + 1]
        line = work[j : j + 1, :]
        pivots = jnp.where(below == j, pivot, pivots)
        if j + 1 < vectors:
            factor = jnp.where(below > j, work[:, j : j + 1] / pivot, 0.0)
            work = work - factor * line
    work = work / jnp.sqrt(pivots)
    beta_out[...] = jnp.where(col_at >= row_at, work[:, :vectors], 0.0)
    next_out[...] = matmul(
        work[:, vectors:], jnp.concatenate([image[...], now[...], prev[...]], axis=0)
    )


def local(rows, cols, tiles, tile_rows, tile_cols, tile_counts, block_now, block_prev, coupling, diag_energy):
    slots, width = tiles.shape[2], tiles.shape[4]
    vectors, piece = block_now.shape
    piece_tiles = piece // width
    planes = cols // 2
    f32 = jnp.float32
    piece_shape = jax.ShapeDtypeStruct((vectors, piece), f32)

    def along_col(x, s):
        return lax.ppermute(x, "col", [(i, i ^ s) for i in range(cols)])

    def along_row(x, s):
        return lax.ppermute(x, "row", [(i, (i - s) % rows) for i in range(rows)])

    def apart(x, s):
        pairs = []
        for r in range(rows):
            for c in range(cols):
                if c % 2 == 0:
                    to = (r, c ^ (2 * s) if s < planes else c)
                else:
                    to = ((r - s) % rows if s < rows else r, c)
                pairs.append((r * cols + c, to[0] * cols + to[1]))
        return lax.ppermute(x, ("row", "col"), pairs)

    in_vmem = pl.BlockSpec(memory_space=VMEM)
    in_hbm = pl.BlockSpec(memory_space=pltpu.HBM)

    def stay(x):
        return pltpu.with_memory_space_constraint(x, pltpu.HBM)

    fixed = pl.pallas_call(
        fixed_kernel,
        out_shape=jax.ShapeDtypeStruct((2 * vectors, 2 * vectors), f32),
        in_specs=[in_hbm] * 2,
        out_specs=in_vmem,
        scratch_shapes=[
            VMEM((2 * vectors, piece), f32),
            pltpu.SemaphoreType.DMA((2,)),
        ],
        compiler_params=pltpu.CompilerParams(vmem_limit_bytes=16 * MIB),
        cost_estimate=pl.CostEstimate(
            flops=WAIT_FLOPS, bytes_accessed=2 * vectors * piece * 4, transcendentals=0
        ),
        name="fixed",
    )(stay(block_now), stay(block_prev))
    beside = along_col(block_now, 1)
    chip = jnp.concatenate([block_now, beside], axis=0)
    peers = range(1, max(planes, rows))
    fetched = [apart(chip, s) for s in peers]
    fetched[0], fixed = lax.optimization_barrier((fetched[0], fixed))
    passed = [along_col(x, 1) for x in fetched]

    group = math.gcd(slots, GROUP)

    keep, send, col_parts = pl.pallas_call(
        functools.partial(products_kernel, rows, planes, group),
        out_shape=(
            jax.ShapeDtypeStruct((planes, vectors, piece), f32),
            jax.ShapeDtypeStruct((planes, vectors, piece), f32),
            jax.ShapeDtypeStruct((rows, vectors, piece), f32),
        ),
        in_specs=[pl.BlockSpec(memory_space=SMEM)]
        + [in_vmem]
        + [in_hbm] * 3
        + [in_vmem] * (1 + 2 * len(peers)),
        out_specs=(in_vmem,) * 3,
        scratch_shapes=[
            SMEM(tile_rows.shape, jnp.int32),
            SMEM(tile_cols.shape, jnp.int32),
            VMEM((1, piece), f32),
            VMEM((cols * piece_tiles, 2 * vectors, width), jnp.bfloat16),
            VMEM((rows * piece_tiles, 2 * vectors, width), jnp.bfloat16),
            VMEM((cols * piece_tiles + 1, vectors, width), f32),
            VMEM((rows * piece_tiles + 1, vectors, width), f32),
            pltpu.SemaphoreType.DMA((3,)),
        ],
        compiler_params=pltpu.CompilerParams(vmem_limit_bytes=20 * MIB),
        name="products",
    )(
        tile_counts,
        pltpu.with_memory_space_constraint(tiles.reshape(slots, width, width), VMEM),
        stay(tile_rows),
        stay(tile_cols),
        stay(diag_energy.reshape(1, piece)),
        chip,
        *fetched,
        *passed,
    )

    back_rows = [along_row(col_parts[s], s) for s in range(1, rows)]
    from_core = along_col(send, 1)
    summed = [keep[s] + from_core[s] for s in range(1, planes)]
    back_planes = [along_col(summed[s - 1], 2 * s) for s in range(1, planes)]
    terms = [keep[0], from_core[0], col_parts[0], *back_planes, *back_rows]

    devices = rows * cols
    image, sums = pl.pallas_call(
        functools.partial(image_kernel, devices),
        out_shape=(
            piece_shape,
            jax.ShapeDtypeStruct((devices, vectors // 2, 128), f32),
        ),
        in_specs=[in_vmem] * (3 + len(terms)),
        out_specs=(in_vmem,) * 2,
        compiler_params=pltpu.CompilerParams(vmem_limit_bytes=16 * MIB),
        name="image",
    )(block_now, block_prev, fixed, *terms)

    sums = lax.all_to_all(sums, ("row", "col"), 0, 0)
    return pl.pallas_call(
        functools.partial(finish_kernel, float(piece * devices)),
        out_shape=(
            piece_shape,
            jax.ShapeDtypeStruct((vectors, vectors), f32),
            jax.ShapeDtypeStruct((vectors, vectors), f32),
        ),
        in_specs=[in_vmem] * 5,
        out_specs=(in_vmem,) * 3,
        compiler_params=pltpu.CompilerParams(vmem_limit_bytes=16 * MIB),
        name="finish",
    )(sums, image, block_now, block_prev, coupling)


def solution(mesh):
    return jax.shard_map(
        functools.partial(local, mesh.shape["row"], mesh.shape["col"]),
        mesh=mesh,
        in_specs=(
            P("row", "col", None, None, None),
            P("row", "col", None),
            P("row", "col", None),
            P("row", "col"),
            P(None, ("row", "col")),
            P(None, ("row", "col")),
            P(),
            P(("row", "col")),
        ),
        out_specs=(P(None, ("row", "col")), P(), P()),
        check_vma=False,
    )
```

```python
import functools
import math

import jax
import jax.numpy as jnp
from jax import lax
from jax.experimental import pallas as pl
from jax.experimental.pallas import tpu as pltpu
from jax.sharding import PartitionSpec as P

VMEM = pltpu.VMEM
SMEM = pltpu.SMEM
GROUP = 128
WAIT_FLOPS = 20_000_000_000
MIB = 1 << 20


def halves(x):
    high = x.astype(jnp.bfloat16)
    low = (x - high.astype(jnp.float32)).astype(jnp.bfloat16)
    return high, low


def contract(left, right):
    return lax.dot_general(
        left,
        right,
        (((1,), (1,)), ((), ())),
        precision=lax.Precision.HIGHEST,
        preferred_element_type=jnp.float32,
    )


def matmul(left, right):
    return jnp.dot(
        left, right, precision=lax.Precision.HIGHEST, preferred_element_type=jnp.float32
    )


def products_kernel(rows, planes, group, *refs):
    peers = max(planes, rows) - 1
    count, tiles, row_idx_hbm, col_idx_hbm, diag_hbm, chip = refs[:6]
    fetched = refs[6 : 6 + peers]
    passed = refs[6 + peers : 6 + 2 * peers]
    (
        keep_out,
        send_out,
        col_out,
        row_idx,
        col_idx,
        diag,
        vec_rows,
        vec_cols,
        acc_rows,
        acc_cols,
        small_sems,
    ) = refs[6 + 2 * peers :]
    row = lax.axis_index("row")
    col = lax.axis_index("col")
    plane, core = col // 2, col % 2
    vectors = chip.shape[0] // 2
    width = tiles.shape[-1]
    piece_tiles = chip.shape[1] // width
    first = core == 0

    small = [
        pltpu.make_async_copy(source, target, small_sems.at[k])
        for k, (source, target) in enumerate(
            (
                (row_idx_hbm, row_idx),
                (col_idx_hbm, col_idx),
                (diag_hbm, diag),
            )
        )
    ]

    total = count[0, 0]
    groups = (total + group - 1) // group

    for copy in small:
        copy.start()
    acc_rows[...] = jnp.zeros_like(acc_rows)
    acc_cols[...] = jnp.zeros_like(acc_cols)

    def store_split(target, base, read):
        for t in range(piece_tiles):
            high, low = halves(read(slice(t * width, (t + 1) * width)))
            target[base + t] = jnp.concatenate([high, low], axis=0)

    for s in range(1, planes):
        base = jnp.bitwise_xor(plane, s) * 2 * piece_tiles
        for side in range(2):
            part = slice(side * vectors, (side + 1) * vectors)
            store_split(
                vec_rows,
                base + side * piece_tiles,
                lambda at: jnp.where(first, fetched[s - 1][part, at], passed[s - 1][part, at]),
            )
    for s in range(1, rows):
        store_split(
            vec_cols,
            lax.rem(row + s, rows) * piece_tiles,
            lambda at: jnp.where(
                first, passed[s - 1][vectors:, at], fetched[s - 1][:vectors, at]
            ),
        )
    store_split(vec_rows, col * piece_tiles, lambda at: chip[:vectors, at])
    store_split(vec_rows, (col + 1 - 2 * core) * piece_tiles, lambda at: chip[vectors:, at])
    store_split(vec_cols, row * piece_tiles, lambda at: chip[:vectors, at])
    small[0].wait()
    small[1].wait()

    spare_row = acc_rows.shape[0] - 1
    spare_col = acc_cols.shape[0] - 1

    def multiply(g, carry):
        for k in range(group):
            m = g * group + k
            alive = m < total
            r, c = row_idx[0, 0, m], col_idx[0, 0, m]
            high, low = halves(tiles[m])
            from_row = vec_rows[r]
            from_col = vec_cols[c]
            back = jnp.dot(
                jnp.concatenate([from_row, from_row], axis=1),
                jnp.concatenate([high, low], axis=0),
                preferred_element_type=jnp.float32,
            )
            ahead = lax.dot_general(
                jnp.concatenate([high, low], axis=1),
                jnp.concatenate([from_col, from_col], axis=1),
                (((1,), (1,)), ((), ())),
                preferred_element_type=jnp.float32,
            ).T
            acc_rows[jnp.where(alive, r, spare_row)] += ahead[:8] + ahead[8:]
            acc_cols[jnp.where(alive, c, spare_col)] += back[:8] + back[8:]
        return carry

    lax.fori_loop(0, groups, multiply, 0)
    small[2].wait()

    for s in range(planes):
        base = jnp.bitwise_xor(plane, s) * 2 * piece_tiles
        for t in range(piece_tiles):
            at = slice(t * width, (t + 1) * width)
            keep_out[s, :, at] = acc_rows[base + core * piece_tiles + t]
            send_out[s, :, at] = acc_rows[base + (1 - core) * piece_tiles + t]
    for s in range(rows):
        base = lax.rem(row + rows - s, rows) * piece_tiles
        for t in range(piece_tiles):
            at = slice(t * width, (t + 1) * width)
            piece = acc_cols[base + t]
            if s == 0:
                piece = piece + chip[:vectors, at] * diag[:, at]
            col_out[s, :, at] = piece


def fixed_kernel(now, prev, out, both, sems):
    vectors = now.shape[0]
    copies = [
        pltpu.make_async_copy(now, both.at[pl.ds(0, vectors)], sems.at[0]),
        pltpu.make_async_copy(prev, both.at[pl.ds(vectors, vectors)], sems.at[1]),
    ]
    for copy in copies:
        copy.start()
    for copy in copies:
        copy.wait()
    out[...] = contract(both[...], both[...])


def image_kernel(copies, *refs):
    now, prev, fixed_in = refs[:3]
    image_out, sums_out = refs[-2:]
    image = refs[3][...]
    for ref in refs[4:-2]:
        image = image + ref[...]
    image_out[...] = image
    block, last = now[...], prev[...]
    vectors = image.shape[0]
    both = jnp.concatenate([block, last], axis=0)
    against = contract(image, jnp.concatenate([image, both], axis=0))
    fixed = fixed_in[...]
    half = sums_out.shape[2] // 2
    used = against.shape[1] + 2 * fixed.shape[1]
    sums = jnp.concatenate(
        [
            against,
            fixed[:vectors],
            fixed[vectors:],
            jnp.zeros((vectors, half - used), jnp.float32),
        ],
        axis=1,
    )
    sums = jnp.concatenate([sums[: vectors // 2], sums[vectors // 2 :]], axis=1)
    for k in range(copies):
        sums_out[k] = sums


def finish_kernel(states, sums_in, image, now, prev, coupling, next_out, alpha_out, beta_out):
    vectors = image.shape[0]
    sums = jnp.sum(sums_in[...], axis=0) / states
    half = sums.shape[1] // 2
    sums = jnp.concatenate([sums[:, :half], sums[:, half:]], axis=0)
    image_gram = sums[:, :vectors]
    alpha_t = sums[:, vectors : 2 * vectors]
    image_prev = sums[:, 2 * vectors : 3 * vectors]
    fixed = jnp.concatenate(
        [sums[:, 3 * vectors : 5 * vectors], sums[:, 5 * vectors : 7 * vectors]], axis=0
    )
    pair = coupling[...]
    left = jnp.concatenate([alpha_t, pair], axis=1)
    seen = jnp.concatenate([alpha_t, image_prev], axis=1)
    gram = image_gram + contract(
        jnp.concatenate([matmul(left, fixed) - seen, -left], axis=1),
        jnp.concatenate([left, seen], axis=1),
    )
    row_at = lax.broadcasted_iota(jnp.int32, (vectors, vectors), 0)
    col_at = lax.broadcasted_iota(jnp.int32, (vectors, vectors), 1)
    eye = (row_at == col_at).astype(jnp.float32)
    alpha_out[...] = contract(eye, alpha_t)
    work = jnp.concatenate([gram, eye, -left], axis=1)
    below = lax.broadcasted_iota(jnp.int32, (vectors, 1), 0)
    pivots = jnp.zeros((vectors, 1), jnp.float32)
    for j in range(vectors):
        pivot = work[j : j + 1, j : j + 1]
        line = work[j : j + 1, :]
        pivots = jnp.where(below == j, pivot, pivots)
        if j + 1 < vectors:
            factor = jnp.where(below > j, work[:, j : j + 1] / pivot, 0.0)
            work = work - factor * line
    work = work / jnp.sqrt(pivots)
    beta_out[...] = jnp.where(col_at >= row_at, work[:, :vectors], 0.0)
    next_out[...] = matmul(
        work[:, vectors:], jnp.concatenate([image[...], now[...], prev[...]], axis=0)
    )


def local(rows, cols, tiles, tile_rows, tile_cols, tile_counts, block_now, block_prev, coupling, diag_energy):
    slots, width = tiles.shape[2], tiles.shape[4]
    vectors, piece = block_now.shape
    piece_tiles = piece // width
    planes = cols // 2
    f32 = jnp.float32
    piece_shape = jax.ShapeDtypeStruct((vectors, piece), f32)

    def along_col(x, s):
        return lax.ppermute(x, "col", [(i, i ^ s) for i in range(cols)])

    def along_row(x, s):
        return lax.ppermute(x, "row", [(i, (i - s) % rows) for i in range(rows)])

    def apart(x, s):
        pairs = []
        for r in range(rows):
            for c in range(cols):
                if c % 2 == 0:
                    to = (r, c ^ (2 * s) if s < planes else c)
                else:
                    to = ((r - s) % rows if s < rows else r, c)
                pairs.append((r * cols + c, to[0] * cols + to[1]))
        return lax.ppermute(x, ("row", "col"), pairs)

    in_vmem = pl.BlockSpec(memory_space=VMEM)
    in_hbm = pl.BlockSpec(memory_space=pltpu.HBM)

    def stay(x):
        return pltpu.with_memory_space_constraint(x, pltpu.HBM)

    fixed = pl.pallas_call(
        fixed_kernel,
        out_shape=jax.ShapeDtypeStruct((2 * vectors, 2 * vectors), f32),
        in_specs=[in_hbm] * 2,
        out_specs=in_vmem,
        scratch_shapes=[
            VMEM((2 * vectors, piece), f32),
            pltpu.SemaphoreType.DMA((2,)),
        ],
        compiler_params=pltpu.CompilerParams(vmem_limit_bytes=16 * MIB),
        cost_estimate=pl.CostEstimate(
            flops=WAIT_FLOPS, bytes_accessed=2 * vectors * piece * 4, transcendentals=0
        ),
        name="fixed",
    )(stay(block_now), stay(block_prev))
    beside = along_col(block_now, 1)
    chip = jnp.concatenate([block_now, beside], axis=0)
    peers = range(1, max(planes, rows))
    fetched = [apart(chip, s) for s in peers]
    fetched[0], fixed = lax.optimization_barrier((fetched[0], fixed))
    passed = [along_col(x, 1) for x in fetched]

    group = math.gcd(slots, GROUP)

    keep, send, col_parts = pl.pallas_call(
        functools.partial(products_kernel, rows, planes, group),
        out_shape=(
            jax.ShapeDtypeStruct((planes, vectors, piece), f32),
            jax.ShapeDtypeStruct((planes, vectors, piece), f32),
            jax.ShapeDtypeStruct((rows, vectors, piece), f32),
        ),
        in_specs=[pl.BlockSpec(memory_space=SMEM)]
        + [in_vmem]
        + [in_hbm] * 3
        + [in_vmem] * (1 + 2 * len(peers)),
        out_specs=(in_vmem,) * 3,
        scratch_shapes=[
            SMEM(tile_rows.shape, jnp.int32),
            SMEM(tile_cols.shape, jnp.int32),
            VMEM((1, piece), f32),
            VMEM((cols * piece_tiles, 2 * vectors, width), jnp.bfloat16),
            VMEM((rows * piece_tiles, 2 * vectors, width), jnp.bfloat16),
            VMEM((cols * piece_tiles + 1, vectors, width), f32),
            VMEM((rows * piece_tiles + 1, vectors, width), f32),
            pltpu.SemaphoreType.DMA((3,)),
        ],
        compiler_params=pltpu.CompilerParams(vmem_limit_bytes=20 * MIB),
        name="products",
    )(
        tile_counts,
        pltpu.with_memory_space_constraint(tiles.reshape(slots, width, width), VMEM),
        stay(tile_rows),
        stay(tile_cols),
        stay(diag_energy.reshape(1, piece)),
        chip,
        *fetched,
        *passed,
    )

    back_rows = [along_row(col_parts[s], s) for s in range(1, rows)]
    from_core = along_col(send, 1)
    summed = [keep[s] + from_core[s] for s in range(1, planes)]
    back_planes = [along_col(summed[s - 1], 2 * s) for s in range(1, planes)]
    terms = [keep[0], from_core[0], col_parts[0], *back_planes, *back_rows]

    devices = rows * cols
    image, sums = pl.pallas_call(
        functools.partial(image_kernel, devices),
        out_shape=(
            piece_shape,
            jax.ShapeDtypeStruct((devices, vectors // 2, 128), f32),
        ),
        in_specs=[in_vmem] * (3 + len(terms)),
        out_specs=(in_vmem,) * 2,
        compiler_params=pltpu.CompilerParams(vmem_limit_bytes=16 * MIB),
        name="image",
    )(block_now, block_prev, fixed, *terms)

    sums = lax.all_to_all(sums, ("row", "col"), 0, 0)
    return pl.pallas_call(
        functools.partial(finish_kernel, float(piece * devices)),
        out_shape=(
            piece_shape,
            jax.ShapeDtypeStruct((vectors, vectors), f32),
            jax.ShapeDtypeStruct((vectors, vectors), f32),
        ),
        in_specs=[in_vmem] * 5,
        out_specs=(in_vmem,) * 3,
        compiler_params=pltpu.CompilerParams(vmem_limit_bytes=16 * MIB),
        name="finish",
    )(sums, image, block_now, block_prev, coupling)


def solution(mesh):
    return jax.shard_map(
        functools.partial(local, mesh.shape["row"], mesh.shape["col"]),
        mesh=mesh,
        in_specs=(
            P("row", "col", None, None, None),
            P("row", "col", None),
            P("row", "col", None),
            P("row", "col"),
            P(None, ("row", "col")),
            P(None, ("row", "col")),
            P(),
            P(("row", "col")),
        ),
        out_specs=(P(None, ("row", "col")), P(), P()),
        check_vma=False,
    )
```

```python
import functools
import math

import jax
import jax.numpy as jnp
from jax import lax
from jax.experimental import pallas as pl
from jax.experimental.pallas import tpu as pltpu
from jax.sharding import PartitionSpec as P

VMEM = pltpu.VMEM
SMEM = pltpu.SMEM
GROUP = 256
WAIT_FLOPS = 20_000_000_000
MIB = 1 << 20


def halves(x):
    high = x.astype(jnp.bfloat16)
    low = (x - high.astype(jnp.float32)).astype(jnp.bfloat16)
    return high, low


def contract(left, right):
    return lax.dot_general(
        left,
        right,
        (((1,), (1,)), ((), ())),
        precision=lax.Precision.HIGHEST,
        preferred_element_type=jnp.float32,
    )


def matmul(left, right):
    return jnp.dot(
        left, right, precision=lax.Precision.HIGHEST, preferred_element_type=jnp.float32
    )


def products_kernel(rows, planes, group, *refs):
    peers = max(planes, rows) - 1
    count, tiles, row_idx_hbm, col_idx_hbm, diag_hbm, chip = refs[:6]
    fetched = refs[6 : 6 + peers]
    passed = refs[6 + peers : 6 + 2 * peers]
    (
        keep_out,
        send_out,
        col_out,
        row_idx,
        col_idx,
        diag,
        vec_rows,
        vec_cols,
        acc_rows,
        acc_cols,
        small_sems,
    ) = refs[6 + 2 * peers :]
    row = lax.axis_index("row")
    col = lax.axis_index("col")
    plane, core = col // 2, col % 2
    vectors = chip.shape[0] // 2
    width = tiles.shape[-1]
    piece_tiles = chip.shape[1] // width
    first = core == 0

    small = [
        pltpu.make_async_copy(source, target, small_sems.at[k])
        for k, (source, target) in enumerate(
            (
                (row_idx_hbm, row_idx),
                (col_idx_hbm, col_idx),
                (diag_hbm, diag),
            )
        )
    ]

    total = count[0, 0]
    groups = (total + group - 1) // group

    for copy in small:
        copy.start()
    acc_rows[...] = jnp.zeros_like(acc_rows)
    acc_cols[...] = jnp.zeros_like(acc_cols)

    def store_split(target, base, read):
        for t in range(piece_tiles):
            high, low = halves(read(slice(t * width, (t + 1) * width)))
            target[base + t] = jnp.concatenate([high, low], axis=0)

    for s in range(1, planes):
        base = jnp.bitwise_xor(plane, s) * 2 * piece_tiles
        for side in range(2):
            part = slice(side * vectors, (side + 1) * vectors)
            store_split(
                vec_rows,
                base + side * piece_tiles,
                lambda at: jnp.where(first, fetched[s - 1][part, at], passed[s - 1][part, at]),
            )
    for s in range(1, rows):
        store_split(
            vec_cols,
            lax.rem(row + s, rows) * piece_tiles,
            lambda at: jnp.where(
                first, passed[s - 1][vectors:, at], fetched[s - 1][:vectors, at]
            ),
        )
    store_split(vec_rows, col * piece_tiles, lambda at: chip[:vectors, at])
    store_split(vec_rows, (col + 1 - 2 * core) * piece_tiles, lambda at: chip[vectors:, at])
    store_split(vec_cols, row * piece_tiles, lambda at: chip[:vectors, at])
    small[0].wait()
    small[1].wait()

    spare_row = acc_rows.shape[0] - 1
    spare_col = acc_cols.shape[0] - 1

    def multiply(g, carry):
        for k in range(group):
            m = g * group + k
            alive = m < total
            r, c = row_idx[0, 0, m], col_idx[0, 0, m]
            high, low = halves(tiles[m])
            from_row = vec_rows[r]
            from_col = vec_cols[c]
            back = jnp.dot(
                jnp.concatenate([from_row, from_row], axis=1),
                jnp.concatenate([high, low], axis=0),
                preferred_element_type=jnp.float32,
            )
            ahead = lax.dot_general(
                jnp.concatenate([high, low], axis=1),
                jnp.concatenate([from_col, from_col], axis=1),
                (((1,), (1,)), ((), ())),
                preferred_element_type=jnp.float32,
            ).T
            acc_rows[jnp.where(alive, r, spare_row)] += ahead[:8] + ahead[8:]
            acc_cols[jnp.where(alive, c, spare_col)] += back[:8] + back[8:]
        return carry

    lax.fori_loop(0, groups, multiply, 0)
    small[2].wait()

    for s in range(planes):
        base = jnp.bitwise_xor(plane, s) * 2 * piece_tiles
        for t in range(piece_tiles):
            at = slice(t * width, (t + 1) * width)
            keep_out[s, :, at] = acc_rows[base + core * piece_tiles + t]
            send_out[s, :, at] = acc_rows[base + (1 - core) * piece_tiles + t]
    for s in range(rows):
        base = lax.rem(row + rows - s, rows) * piece_tiles
        for t in range(piece_tiles):
            at = slice(t * width, (t + 1) * width)
            piece = acc_cols[base + t]
            if s == 0:
                piece = piece + chip[:vectors, at] * diag[:, at]
            col_out[s, :, at] = piece


def fixed_kernel(now, prev, out, both, sems):
    vectors = now.shape[0]
    copies = [
        pltpu.make_async_copy(now, both.at[pl.ds(0, vectors)], sems.at[0]),
        pltpu.make_async_copy(prev, both.at[pl.ds(vectors, vectors)], sems.at[1]),
    ]
    for copy in copies:
        copy.start()
    for copy in copies:
        copy.wait()
    out[...] = contract(both[...], both[...])


def image_kernel(copies, *refs):
    now, prev, fixed_in = refs[:3]
    image_out, sums_out = refs[-2:]
    image = refs[3][...]
    for ref in refs[4:-2]:
        image = image + ref[...]
    image_out[...] = image
    block, last = now[...], prev[...]
    vectors = image.shape[0]
    both = jnp.concatenate([block, last], axis=0)
    against = contract(image, jnp.concatenate([image, both], axis=0))
    fixed = fixed_in[...]
    half = sums_out.shape[2] // 2
    used = against.shape[1] + 2 * fixed.shape[1]
    sums = jnp.concatenate(
        [
            against,
            fixed[:vectors],
            fixed[vectors:],
            jnp.zeros((vectors, half - used), jnp.float32),
        ],
        axis=1,
    )
    sums = jnp.concatenate([sums[: vectors // 2], sums[vectors // 2 :]], axis=1)
    for k in range(copies):
        sums_out[k] = sums


def finish_kernel(states, sums_in, image, now, prev, coupling, next_out, alpha_out, beta_out):
    vectors = image.shape[0]
    sums = jnp.sum(sums_in[...], axis=0) / states
    half = sums.shape[1] // 2
    sums = jnp.concatenate([sums[:, :half], sums[:, half:]], axis=0)
    image_gram = sums[:, :vectors]
    alpha_t = sums[:, vectors : 2 * vectors]
    image_prev = sums[:, 2 * vectors : 3 * vectors]
    fixed = jnp.concatenate(
        [sums[:, 3 * vectors : 5 * vectors], sums[:, 5 * vectors : 7 * vectors]], axis=0
    )
    pair = coupling[...]
    left = jnp.concatenate([alpha_t, pair], axis=1)
    seen = jnp.concatenate([alpha_t, image_prev], axis=1)
    gram = image_gram + contract(
        jnp.concatenate([matmul(left, fixed) - seen, -left], axis=1),
        jnp.concatenate([left, seen], axis=1),
    )
    row_at = lax.broadcasted_iota(jnp.int32, (vectors, vectors), 0)
    col_at = lax.broadcasted_iota(jnp.int32, (vectors, vectors), 1)
    eye = (row_at == col_at).astype(jnp.float32)
    alpha_out[...] = contract(eye, alpha_t)
    work = jnp.concatenate([gram, eye, -left], axis=1)
    below = lax.broadcasted_iota(jnp.int32, (vectors, 1), 0)
    pivots = jnp.zeros((vectors, 1), jnp.float32)
    for j in range(vectors):
        pivot = work[j : j + 1, j : j + 1]
        line = work[j : j + 1, :]
        pivots = jnp.where(below == j, pivot, pivots)
        if j + 1 < vectors:
            factor = jnp.where(below > j, work[:, j : j + 1] / pivot, 0.0)
            work = work - factor * line
    work = work / jnp.sqrt(pivots)
    beta_out[...] = jnp.where(col_at >= row_at, work[:, :vectors], 0.0)
    next_out[...] = matmul(
        work[:, vectors:], jnp.concatenate([image[...], now[...], prev[...]], axis=0)
    )


def local(rows, cols, tiles, tile_rows, tile_cols, tile_counts, block_now, block_prev, coupling, diag_energy):
    slots, width = tiles.shape[2], tiles.shape[4]
    vectors, piece = block_now.shape
    piece_tiles = piece // width
    planes = cols // 2
    f32 = jnp.float32
    piece_shape = jax.ShapeDtypeStruct((vectors, piece), f32)

    def along_col(x, s):
        return lax.ppermute(x, "col", [(i, i ^ s) for i in range(cols)])

    def along_row(x, s):
        return lax.ppermute(x, "row", [(i, (i - s) % rows) for i in range(rows)])

    def apart(x, s):
        pairs = []
        for r in range(rows):
            for c in range(cols):
                if c % 2 == 0:
                    to = (r, c ^ (2 * s) if s < planes else c)
                else:
                    to = ((r - s) % rows if s < rows else r, c)
                pairs.append((r * cols + c, to[0] * cols + to[1]))
        return lax.ppermute(x, ("row", "col"), pairs)

    in_vmem = pl.BlockSpec(memory_space=VMEM)
    in_hbm = pl.BlockSpec(memory_space=pltpu.HBM)

    def stay(x):
        return pltpu.with_memory_space_constraint(x, pltpu.HBM)

    fixed = pl.pallas_call(
        fixed_kernel,
        out_shape=jax.ShapeDtypeStruct((2 * vectors, 2 * vectors), f32),
        in_specs=[in_hbm] * 2,
        out_specs=in_vmem,
        scratch_shapes=[
            VMEM((2 * vectors, piece), f32),
            pltpu.SemaphoreType.DMA((2,)),
        ],
        compiler_params=pltpu.CompilerParams(vmem_limit_bytes=16 * MIB),
        cost_estimate=pl.CostEstimate(
            flops=WAIT_FLOPS, bytes_accessed=2 * vectors * piece * 4, transcendentals=0
        ),
        name="fixed",
    )(stay(block_now), stay(block_prev))
    beside = along_col(block_now, 1)
    chip = jnp.concatenate([block_now, beside], axis=0)
    peers = range(1, max(planes, rows))
    fetched = [apart(chip, s) for s in peers]
    fetched[0], fixed = lax.optimization_barrier((fetched[0], fixed))
    passed = [along_col(x, 1) for x in fetched]

    group = math.gcd(slots, GROUP)

    keep, send, col_parts = pl.pallas_call(
        functools.partial(products_kernel, rows, planes, group),
        out_shape=(
            jax.ShapeDtypeStruct((planes, vectors, piece), f32),
            jax.ShapeDtypeStruct((planes, vectors, piece), f32),
            jax.ShapeDtypeStruct((rows, vectors, piece), f32),
        ),
        in_specs=[pl.BlockSpec(memory_space=SMEM)]
        + [in_vmem]
        + [in_hbm] * 3
        + [in_vmem] * (1 + 2 * len(peers)),
        out_specs=(in_vmem,) * 3,
        scratch_shapes=[
            SMEM(tile_rows.shape, jnp.int32),
            SMEM(tile_cols.shape, jnp.int32),
            VMEM((1, piece), f32),
            VMEM((cols * piece_tiles, 2 * vectors, width), jnp.bfloat16),
            VMEM((rows * piece_tiles, 2 * vectors, width), jnp.bfloat16),
            VMEM((cols * piece_tiles + 1, vectors, width), f32),
            VMEM((rows * piece_tiles + 1, vectors, width), f32),
            pltpu.SemaphoreType.DMA((3,)),
        ],
        compiler_params=pltpu.CompilerParams(vmem_limit_bytes=20 * MIB),
        name="products",
    )(
        tile_counts,
        pltpu.with_memory_space_constraint(tiles.reshape(slots, width, width), VMEM),
        stay(tile_rows),
        stay(tile_cols),
        stay(diag_energy.reshape(1, piece)),
        chip,
        *fetched,
        *passed,
    )

    back_rows = [along_row(col_parts[s], s) for s in range(1, rows)]
    from_core = along_col(send, 1)
    summed = [keep[s] + from_core[s] for s in range(1, planes)]
    back_planes = [along_col(summed[s - 1], 2 * s) for s in range(1, planes)]
    terms = [keep[0], from_core[0], col_parts[0], *back_planes, *back_rows]

    devices = rows * cols
    image, sums = pl.pallas_call(
        functools.partial(image_kernel, devices),
        out_shape=(
            piece_shape,
            jax.ShapeDtypeStruct((devices, vectors // 2, 128), f32),
        ),
        in_specs=[in_vmem] * (3 + len(terms)),
        out_specs=(in_vmem,) * 2,
        compiler_params=pltpu.CompilerParams(vmem_limit_bytes=16 * MIB),
        name="image",
    )(block_now, block_prev, fixed, *terms)

    sums = lax.all_to_all(sums, ("row", "col"), 0, 0)
    return pl.pallas_call(
        functools.partial(finish_kernel, float(piece * devices)),
        out_shape=(
            piece_shape,
            jax.ShapeDtypeStruct((vectors, vectors), f32),
            jax.ShapeDtypeStruct((vectors, vectors), f32),
        ),
        in_specs=[in_vmem] * 5,
        out_specs=(in_vmem,) * 3,
        compiler_params=pltpu.CompilerParams(vmem_limit_bytes=16 * MIB),
        name="finish",
    )(sums, image, block_now, block_prev, coupling)


def solution(mesh):
    return jax.shard_map(
        functools.partial(local, mesh.shape["row"], mesh.shape["col"]),
        mesh=mesh,
        in_specs=(
            P("row", "col", None, None, None),
            P("row", "col", None),
            P("row", "col", None),
            P("row", "col"),
            P(None, ("row", "col")),
            P(None, ("row", "col")),
            P(),
            P(("row", "col")),
        ),
        out_specs=(P(None, ("row", "col")), P(), P()),
        check_vma=False,
    )
```

```python
import functools
import math

import jax
import jax.numpy as jnp
from jax import lax
from jax.experimental import pallas as pl
from jax.experimental.pallas import tpu as pltpu
from jax.sharding import PartitionSpec as P

VMEM = pltpu.VMEM
SMEM = pltpu.SMEM
GROUP = 128
WAIT_FLOPS = 20_000_000_000
MIB = 1 << 20


def halves(x):
    high = x.astype(jnp.bfloat16)
    low = (x - high.astype(jnp.float32)).astype(jnp.bfloat16)
    return high, low


def contract(left, right):
    return lax.dot_general(
        left,
        right,
        (((1,), (1,)), ((), ())),
        precision=lax.Precision.HIGHEST,
        preferred_element_type=jnp.float32,
    )


def matmul(left, right):
    return jnp.dot(
        left, right, precision=lax.Precision.HIGHEST, preferred_element_type=jnp.float32
    )


def products_kernel(rows, planes, group, *refs):
    peers = max(planes, rows) - 1
    count, tiles, row_idx_hbm, col_idx_hbm, diag_hbm, chip = refs[:6]
    fetched = refs[6 : 6 + peers]
    passed = refs[6 + peers : 6 + 2 * peers]
    (
        keep_out,
        send_out,
        col_out,
        row_idx,
        col_idx,
        diag,
        vec_rows,
        vec_cols,
        acc_rows,
        acc_cols,
        small_sems,
    ) = refs[6 + 2 * peers :]
    row = lax.axis_index("row")
    col = lax.axis_index("col")
    plane, core = col // 2, col % 2
    vectors = chip.shape[0] // 2
    width = tiles.shape[-1]
    piece_tiles = chip.shape[1] // width
    first = core == 0

    small = [
        pltpu.make_async_copy(source, target, small_sems.at[k])
        for k, (source, target) in enumerate(
            (
                (row_idx_hbm, row_idx),
                (col_idx_hbm, col_idx),
                (diag_hbm, diag),
            )
        )
    ]

    total = count[0, 0]
    groups = (total + group - 1) // group

    for copy in small:
        copy.start()
    acc_rows[...] = jnp.zeros_like(acc_rows)
    acc_cols[...] = jnp.zeros_like(acc_cols)

    def store_split(target, base, read):
        for t in range(piece_tiles):
            high, low = halves(read(slice(t * width, (t + 1) * width)))
            target[base + t] = jnp.concatenate([high, low], axis=0)

    for s in range(1, planes):
        base = jnp.bitwise_xor(plane, s) * 2 * piece_tiles
        for side in range(2):
            part = slice(side * vectors, (side + 1) * vectors)
            store_split(
                vec_rows,
                base + side * piece_tiles,
                lambda at: jnp.where(first, fetched[s - 1][part, at], passed[s - 1][part, at]),
            )
    for s in range(1, rows):
        store_split(
            vec_cols,
            lax.rem(row + s, rows) * piece_tiles,
            lambda at: jnp.where(
                first, passed[s - 1][vectors:, at], fetched[s - 1][:vectors, at]
            ),
        )
    store_split(vec_rows, col * piece_tiles, lambda at: chip[:vectors, at])
    store_split(vec_rows, (col + 1 - 2 * core) * piece_tiles, lambda at: chip[vectors:, at])
    store_split(vec_cols, row * piece_tiles, lambda at: chip[:vectors, at])
    small[0].wait()
    small[1].wait()

    spare_row = acc_rows.shape[0] - 1
    spare_col = acc_cols.shape[0] - 1

    def multiply(g, carry):
        for k in range(group):
            m = g * group + k
            alive = m < total
            r, c = row_idx[0, 0, m], col_idx[0, 0, m]
            high, low = halves(tiles[m])
            from_row = vec_rows[r]
            from_col = vec_cols[c]
            back = jnp.dot(
                jnp.concatenate([from_row, from_row], axis=1),
                jnp.concatenate([high, low], axis=0),
                preferred_element_type=jnp.float32,
            )
            ahead = lax.dot_general(
                jnp.concatenate([high, low], axis=1),
                jnp.concatenate([from_col, from_col], axis=1),
                (((1,), (1,)), ((), ())),
                preferred_element_type=jnp.float32,
            ).T
            acc_rows[jnp.where(alive, r, spare_row)] += ahead[:8] + ahead[8:]
            acc_cols[jnp.where(alive, c, spare_col)] += back[:8] + back[8:]
        return carry

    lax.fori_loop(0, groups, multiply, 0)
    small[2].wait()

    for s in range(planes):
        base = jnp.bitwise_xor(plane, s) * 2 * piece_tiles
        for t in range(piece_tiles):
            at = slice(t * width, (t + 1) * width)
            keep_out[s, :, at] = acc_rows[base + core * piece_tiles + t]
            send_out[s, :, at] = acc_rows[base + (1 - core) * piece_tiles + t]
    for s in range(rows):
        base = lax.rem(row + rows - s, rows) * piece_tiles
        for t in range(piece_tiles):
            at = slice(t * width, (t + 1) * width)
            piece = acc_cols[base + t]
            if s == 0:
                piece = piece + chip[:vectors, at] * diag[:, at]
            col_out[s, :, at] = piece


def fixed_kernel(now, prev, out, both, sems):
    vectors = now.shape[0]
    copies = [
        pltpu.make_async_copy(now, both.at[pl.ds(0, vectors)], sems.at[0]),
        pltpu.make_async_copy(prev, both.at[pl.ds(vectors, vectors)], sems.at[1]),
    ]
    for copy in copies:
        copy.start()
    for copy in copies:
        copy.wait()
    out[...] = contract(both[...], both[...])


def image_kernel(copies, *refs):
    now, prev, fixed_in = refs[:3]
    image_out, sums_out = refs[-2:]
    image = refs[3][...]
    for ref in refs[4:-2]:
        image = image + ref[...]
    image_out[...] = image
    block, last = now[...], prev[...]
    vectors = image.shape[0]
    both = jnp.concatenate([block, last], axis=0)
    against = contract(image, jnp.concatenate([image, both], axis=0))
    fixed = fixed_in[...]
    half = sums_out.shape[2] // 2
    used = against.shape[1] + 2 * fixed.shape[1]
    sums = jnp.concatenate(
        [
            against,
            fixed[:vectors],
            fixed[vectors:],
            jnp.zeros((vectors, half - used), jnp.float32),
        ],
        axis=1,
    )
    sums = jnp.concatenate([sums[: vectors // 2], sums[vectors // 2 :]], axis=1)
    for k in range(copies):
        sums_out[k] = sums


def finish_kernel(states, sums_in, image, now, prev, coupling, next_out, alpha_out, beta_out):
    vectors = image.shape[0]
    sums = jnp.sum(sums_in[...], axis=0) / states
    half = sums.shape[1] // 2
    sums = jnp.concatenate([sums[:, :half], sums[:, half:]], axis=0)
    image_gram = sums[:, :vectors]
    alpha_t = sums[:, vectors : 2 * vectors]
    image_prev = sums[:, 2 * vectors : 3 * vectors]
    fixed = jnp.concatenate(
        [sums[:, 3 * vectors : 5 * vectors], sums[:, 5 * vectors : 7 * vectors]], axis=0
    )
    pair = coupling[...]
    left = jnp.concatenate([alpha_t, pair], axis=1)
    seen = jnp.concatenate([alpha_t, image_prev], axis=1)
    gram = image_gram + contract(
        jnp.concatenate([matmul(left, fixed) - seen, -left], axis=1),
        jnp.concatenate([left, seen], axis=1),
    )
    row_at = lax.broadcasted_iota(jnp.int32, (vectors, vectors), 0)
    col_at = lax.broadcasted_iota(jnp.int32, (vectors, vectors), 1)
    eye = (row_at == col_at).astype(jnp.float32)
    alpha_out[...] = contract(eye, alpha_t)
    work = jnp.concatenate([gram, eye, -left], axis=1)
    below = lax.broadcasted_iota(jnp.int32, (vectors, 1), 0)
    pivots = jnp.zeros((vectors, 1), jnp.float32)
    for j in range(vectors):
        pivot = work[j : j + 1, j : j + 1]
        line = work[j : j + 1, :]
        pivots = jnp.where(below == j, pivot, pivots)
        if j + 1 < vectors:
            factor = jnp.where(below > j, work[:, j : j + 1] / pivot, 0.0)
            work = work - factor * line
    work = work / jnp.sqrt(pivots)
    beta_out[...] = jnp.where(col_at >= row_at, work[:, :vectors], 0.0)
    next_out[...] = matmul(
        work[:, vectors:], jnp.concatenate([image[...], now[...], prev[...]], axis=0)
    )


def local(rows, cols, tiles, tile_rows, tile_cols, tile_counts, block_now, block_prev, coupling, diag_energy):
    slots, width = tiles.shape[2], tiles.shape[4]
    vectors, piece = block_now.shape
    piece_tiles = piece // width
    planes = cols // 2
    f32 = jnp.float32
    piece_shape = jax.ShapeDtypeStruct((vectors, piece), f32)

    def along_col(x, s):
        return lax.ppermute(x, "col", [(i, i ^ s) for i in range(cols)])

    def along_row(x, s):
        return lax.ppermute(x, "row", [(i, (i - s) % rows) for i in range(rows)])

    def apart(x, s):
        pairs = []
        for r in range(rows):
            for c in range(cols):
                if c % 2 == 0:
                    to = (r, c ^ (2 * s) if s < planes else c)
                else:
                    to = ((r - s) % rows if s < rows else r, c)
                pairs.append((r * cols + c, to[0] * cols + to[1]))
        return lax.ppermute(x, ("row", "col"), pairs)

    in_vmem = pl.BlockSpec(memory_space=VMEM)
    in_hbm = pl.BlockSpec(memory_space=pltpu.HBM)

    def stay(x):
        return pltpu.with_memory_space_constraint(x, pltpu.HBM)

    fixed = pl.pallas_call(
        fixed_kernel,
        out_shape=jax.ShapeDtypeStruct((2 * vectors, 2 * vectors), f32),
        in_specs=[in_hbm] * 2,
        out_specs=in_vmem,
        scratch_shapes=[
            VMEM((2 * vectors, piece), f32),
            pltpu.SemaphoreType.DMA((2,)),
        ],
        compiler_params=pltpu.CompilerParams(vmem_limit_bytes=16 * MIB),
        cost_estimate=pl.CostEstimate(
            flops=WAIT_FLOPS, bytes_accessed=2 * vectors * piece * 4, transcendentals=0
        ),
        name="fixed",
    )(stay(block_now), stay(block_prev))
    beside = along_col(block_now, 1)
    chip = jnp.concatenate([block_now, beside], axis=0)
    peers = range(1, max(planes, rows))
    fetched = [apart(chip, s) for s in peers]
    fetched[0], fixed = lax.optimization_barrier((fetched[0], fixed))
    passed = [along_col(x, 1) for x in fetched]

    group = math.gcd(slots, GROUP)

    keep, send, col_parts = pl.pallas_call(
        functools.partial(products_kernel, rows, planes, group),
        out_shape=(
            jax.ShapeDtypeStruct((planes, vectors, piece), f32),
            jax.ShapeDtypeStruct((planes, vectors, piece), f32),
            jax.ShapeDtypeStruct((rows, vectors, piece), f32),
        ),
        in_specs=[pl.BlockSpec(memory_space=SMEM)]
        + [in_vmem]
        + [in_hbm] * 3
        + [in_vmem] * (1 + 2 * len(peers)),
        out_specs=(in_vmem,) * 3,
        scratch_shapes=[
            SMEM(tile_rows.shape, jnp.int32),
            SMEM(tile_cols.shape, jnp.int32),
            VMEM((1, piece), f32),
            VMEM((cols * piece_tiles, 2 * vectors, width), jnp.bfloat16),
            VMEM((rows * piece_tiles, 2 * vectors, width), jnp.bfloat16),
            VMEM((cols * piece_tiles + 1, vectors, width), f32),
            VMEM((rows * piece_tiles + 1, vectors, width), f32),
            pltpu.SemaphoreType.DMA((3,)),
        ],
        compiler_params=pltpu.CompilerParams(vmem_limit_bytes=20 * MIB),
        name="products",
    )(
        tile_counts,
        pltpu.with_memory_space_constraint(tiles.reshape(slots, width, width), VMEM),
        stay(tile_rows),
        stay(tile_cols),
        stay(diag_energy.reshape(1, piece)),
        chip,
        *fetched,
        *passed,
    )

    back_rows = [along_row(col_parts[s], s) for s in range(1, rows)]
    from_core = along_col(send, 1)
    summed = [keep[s] + from_core[s] for s in range(1, planes)]
    back_planes = [along_col(summed[s - 1], 2 * s) for s in range(1, planes)]
    terms = [keep[0], from_core[0], col_parts[0], *back_planes[::-1], *back_rows]

    devices = rows * cols
    image, sums = pl.pallas_call(
        functools.partial(image_kernel, devices),
        out_shape=(
            piece_shape,
            jax.ShapeDtypeStruct((devices, vectors // 2, 128), f32),
        ),
        in_specs=[in_vmem] * (3 + len(terms)),
        out_specs=(in_vmem,) * 2,
        compiler_params=pltpu.CompilerParams(vmem_limit_bytes=16 * MIB),
        name="image",
    )(block_now, block_prev, fixed, *terms)

    sums = lax.all_to_all(sums, ("row", "col"), 0, 0)
    return pl.pallas_call(
        functools.partial(finish_kernel, float(piece * devices)),
        out_shape=(
            piece_shape,
            jax.ShapeDtypeStruct((vectors, vectors), f32),
            jax.ShapeDtypeStruct((vectors, vectors), f32),
        ),
        in_specs=[in_vmem] * 5,
        out_specs=(in_vmem,) * 3,
        compiler_params=pltpu.CompilerParams(vmem_limit_bytes=16 * MIB),
        name="finish",
    )(sums, image, block_now, block_prev, coupling)


def solution(mesh):
    return jax.shard_map(
        functools.partial(local, mesh.shape["row"], mesh.shape["col"]),
        mesh=mesh,
        in_specs=(
            P("row", "col", None, None, None),
            P("row", "col", None),
            P("row", "col", None),
            P("row", "col"),
            P(None, ("row", "col")),
            P(None, ("row", "col")),
            P(),
            P(("row", "col")),
        ),
        out_specs=(P(None, ("row", "col")), P(), P()),
        check_vma=False,
    )
```
